32 devices in a mesh: lat: 8 (over z, y), lon: 4 (over x, core).
Axes of the slice: x: 2, y: 2, z: 4, core: 2. Of those that a mesh axis runs over, the one named last changes fastest.
Arguments:
- adj_next: float32 [32, 5, 16, 2880], P('lat', None, None, 'lon'), may hold values from -6 to 6
- east_courant: float32 [32, 16, 2880], P('lat', None, 'lon'), may hold values from -0.45 to 0.45
- north_courant: float32 [32, 16, 2880], P('lat', None, 'lon'), may hold values from -0.45 to 0.45
- cutoff: int32 [2, 4], replicated, may hold values from 1 to 351, as said below
Outputs:
- adj_now: float32 [32, 5, 16, 2880], P('lat', None, None, 'lon')
The draws below stay inside these ranges and needn't reach their ends.
Inputs may be any that keep to these rules, and one draw needn't show every extreme that they name: In each cap the latitude nearest the pole has cutoff 1 and the latitude farthest from it has cutoff 352 - 1.
All inputs are finite; a program needn't handle non-finite values.
Results may differ from the reference program's by a relative error of at most 0.0001.
Values sent between devices are 32-bit elements; how exact they have to be, the bound alone decides.
No kernel may reach another device: no remote copies, remote signals or barrier semaphores. Data moves between devices by JAX's collectives and lax.ppermute only.
A program may use at most 64 MiB of HBM per device.

```python
import jax
import jax.numpy as jnp

NLON = 2880
C = 5
LEV = 16
KF = 352
NLAT = 32
CAP_LAT = 4


def draw_cutoff(key, part):
    steps_away = jnp.arange(CAP_LAT, dtype=jnp.int32)
    distances = jnp.stack([steps_away, CAP_LAT - 1 - steps_away])
    baseline = 1 + distances * (KF - 2) // (CAP_LAT - 1)
    jitter = jax.random.randint(key, (2, CAP_LAT), 0, 4)
    values = jnp.maximum(baseline - jitter, 1)
    values = jnp.where(distances == CAP_LAT - 1, KF - 1, values)
    values = jnp.where(distances == 0, 1, values)
    return values.astype(jnp.int32)


def block_scale(rng, dims, cuts, low, largest):
    def one(dim, shards_of):
        draws = jax.random.uniform(jax.random.fold_in(jax.random.fold_in(rng, 6), dim), (shards_of,), jnp.float32, low / len(cuts), largest / len(cuts))
        return jnp.repeat(jnp.exp(draws), dims[dim] // shards_of).reshape((-1,) + (1,) * (len(dims) - dim - 1))

    loudness = one(*cuts[0])
    for cut in cuts[1:]:
        loudness = loudness * one(*cut)
    return loudness


def noise(key, dims, scale, reach, shards=(), kind=jnp.bfloat16):
    entries = jax.random.normal(key, dims, jnp.float32) * scale
    if len(shards) > 0:
        entries = block_scale(key, dims, shards, -0.22, 0.18) * entries
    return jnp.clip(entries, min=-reach, max=reach).astype(kind)


def setup_inputs(seed: int = 0) -> dict:
    splits = jax.random.split(jax.random.key(seed), 5)
    return {
        "adj_next": noise(splits[0], (NLAT, C, LEV, NLON), 1.0, 6.0, ((0, 8), (3, 4)), jnp.float32),
        "east_courant": jnp.clip(jax.random.uniform(splits[1], (NLAT, LEV, NLON), jnp.float32, -0.45, 0.45) * block_scale(splits[1], (NLAT, LEV, NLON), ((0, 8), (2, 4)), -0.4, 0.0), -0.45, 0.45),
        "north_courant": jnp.clip(jax.random.uniform(splits[2], (NLAT, LEV, NLON), jnp.float32, -0.45, 0.45) * block_scale(splits[2], (NLAT, LEV, NLON), ((0, 8), (2, 4)), -0.4, 0.0), -0.45, 0.45),
        "cutoff": draw_cutoff(jax.random.fold_in(splits[4], 71), 0),
    }


def transpose_step(tracer, east_courant, north_courant):
    zonal_flux = east_courant * tracer
    meridional = north_courant * tracer
    result = tracer + jnp.roll(zonal_flux, -1, axis=2) - jnp.roll(zonal_flux, 1, axis=2)
    zero_row = jnp.zeros_like(meridional[:1])
    from_north = jnp.concatenate([meridional[1:], zero_row], axis=0)
    from_south = jnp.concatenate([zero_row, meridional[:-1]], axis=0)
    result = result + from_north - from_south
    half_turn = NLON // 2
    result = result.at[0].add(jnp.roll(meridional[0], half_turn, axis=1))
    result = result.at[-1].add(-jnp.roll(meridional[-1], half_turn, axis=1))
    return result


def low_pass(rows, chosen):
    spectrum = jnp.fft.rfft(rows, axis=-1)
    wavenumber = jnp.arange(spectrum.shape[-1], dtype=jnp.int32)
    kept_mask = wavenumber[None, None, :] <= chosen[:, None, None]
    spectrum = jnp.where(kept_mask, spectrum, jnp.zeros_like(spectrum))
    return jnp.fft.irfft(spectrum, n=NLON, axis=-1)


def reference(adj_next, east_courant, north_courant, cutoff):
    outputs = []
    for tracer_index in range(C):
        tracer = adj_next[:, tracer_index]
        result = transpose_step(tracer, east_courant, north_courant)
        north_cap = low_pass(result[:CAP_LAT], cutoff[0])
        south_cap = low_pass(result[NLAT - CAP_LAT:], cutoff[1])
        result = jnp.concatenate([north_cap, result[CAP_LAT:NLAT - CAP_LAT], south_cap], axis=0)
        outputs.append(result)
    return jnp.stack(outputs, axis=1)
```

```python
import functools
import math

import jax
import jax.numpy as jnp
import ml_dtypes
import numpy as np
from jax import lax
from jax.experimental import pallas as pl
from jax.experimental.pallas import tpu as pltpu
from jax.sharding import PartitionSpec as P

KF = 352
LANE = 128
VMEM = pltpu.VMEM


def ceil_to(value, unit):
    return -(-value // unit) * unit


def split16(table):
    high = table.astype(ml_dtypes.bfloat16)
    low = (table - high.astype(np.float64)).astype(ml_dtypes.bfloat16)
    return np.stack([high, low])


def tables(cols, circle, lon_count):
    wide = ceil_to(cols + 2, LANE)
    half = ceil_to(KF + 2, LANE)
    place = np.zeros(wide, np.int64)
    place[: cols + 1] = np.arange(cols + 1)
    place[-1] = -1
    live = np.zeros(wide)
    live[: cols + 1] = 1
    live[-1] = 1
    mode = np.arange(KF)
    phase = 2 * np.pi * ((place[:, None] * mode[None]) % circle) / circle
    forward = np.zeros((wide, 2 * half))
    forward[:, :KF] = np.cos(phase) * live[:, None]
    forward[:, half : half + KF] = np.sin(phase) * live[:, None]
    backward = forward.T.copy()
    backward[:, cols:] = 0
    turn = np.zeros((lon_count, 2, half), np.float32)
    angle = 2 * np.pi * ((np.arange(lon_count)[:, None] * mode[None]) % lon_count) / lon_count
    turn[:, 0, :KF] = np.cos(angle)
    turn[:, 1, :KF] = np.sin(angle)
    pole = np.zeros((lon_count, 4, wide), np.float32)
    for index in range(lon_count):
        first = 2 * np.pi * (place + index * cols) / circle
        pole[index, 0] = live
        pole[index, 1] = np.cos(first) * live
        pole[index, 2] = np.sin(first) * live
    return split16(forward), split16(backward), turn, pole


def dot3(block, table_ref):
    high = block.astype(jnp.bfloat16)
    low = (block - high.astype(jnp.float32)).astype(jnp.bfloat16)
    total = jnp.dot(high, table_ref[0], preferred_element_type=jnp.float32)
    total += jnp.dot(high, table_ref[1], preferred_element_type=jnp.float32)
    return total + jnp.dot(low, table_ref[0], preferred_element_type=jnp.float32)


def roles(lat_count):
    lat = lax.axis_index("lat")
    last = lat_count - 1
    north, south = lat == 0, lat == last
    polar = jnp.logical_or(north, south)
    beside = jnp.logical_or(lat == 1, lat == last - 1)
    even = lax.rem(lat, 2) == 0
    return south, polar, beside, even


def local_kernel(lat_count, adj, east, north, fwd, turn, pole, base, edge_a, edge_b, sides, keep, send, flux, wide_x):
    rows, tracers, levels, cols = adj.shape
    wide = flux.shape[-1]
    south, polar, beside, even = roles(lat_count)
    lon = lax.axis_index("lon")
    core = lax.rem(lon, 2)
    half_lev = levels // 2
    half = fwd.shape[-1] // 2
    row_a = jnp.where(even, rows - 1, 0)
    row_b = rows - 1 - row_a
    edge_a[...] = north[row_a][None] * adj[row_a]
    edge_b[...] = north[row_b][None] * adj[row_b]

    pad = jnp.zeros((levels, wide - cols), jnp.float32)

    def transported(r, t):
        out = adj[r, t]
        if r + 1 < rows:
            out = out + north[r + 1] * adj[r + 1, t]
        if r > 0:
            out = out - north[r - 1] * adj[r - 1, t]
        return out

    def spread(r, t):
        flux[:, :cols] = east[r] * adj[r, t]
        f = flux[...]
        return pltpu.roll(f, wide - 1, 1) - pltpu.roll(f, 1, 1), f

    flux[:, cols:] = pad

    def turned(p):
        a, b = turn[lon, 0:1], turn[lon, 1:2]
        c, s = p[:, :half], p[:, half:]
        return c * a - s * b, s * a + c * b

    def put(slot, p):
        c, s = turned(p)
        n = c.shape[0] // 2
        keep[slot, :, :half] = c[:n]
        keep[slot, :, half:] = s[:n]
        send[slot, :, :half] = c[n:]
        send[slot, :, half:] = s[n:]

    @pl.when(jnp.logical_not(polar))
    def _():
        ends = jnp.zeros((8, wide), jnp.float32)
        row = lax.broadcasted_iota(jnp.int32, (8, wide), 0)
        lane = lax.broadcasted_iota(jnp.int32, (8, wide), 1)
        pick = jnp.where((row == 0) & (lane == 0) | (row == 1) & (lane == cols - 1), 1.0, 0.0).astype(jnp.float32)
        for r in range(rows):
            for t in range(tracers):
                move, f = spread(r, t)
                base[r, t] = transported(r, t) + move[:, :cols]
                wide_x[r, 0, t] = f[:half_lev]
                wide_x[r, 1, t] = f[half_lev:]
        whole = wide_x[...].reshape(rows * tracers * levels, wide)
        sides[...] = lax.dot_general(
            pick, whole, (((1,), (1,)), ((), ())), precision=lax.Precision.HIGHEST, preferred_element_type=jnp.float32
        )

    @pl.when(beside)
    def _():
        sign = jnp.where(even, -1.0, 1.0).astype(jnp.float32)
        wide_x[2] = jnp.zeros(wide_x.shape[1:], jnp.float32)
        for t in range(tracers):
            m = edge_a[t] * sign
            wide_x[2, core, t, :, :cols] = m[:half_lev]
            wide_x[2, 1 - core, t, :, :cols] = m[half_lev:]
        put(2, dot3(wide_x[2].reshape(tracers * levels, wide), fwd))

    @pl.when(polar)
    def _():
        for r in range(rows):
            near = jnp.where(south, rows - 1 - r, r)
            slot = lax.rem(near + rows - 1, rows)
            for t in range(tracers):
                move, _ = spread(r, t)
                for h in (0, 1):
                    part = slice(h * half_lev, (h + 1) * half_lev)
                    where = jnp.where(core == 0, h, 1 - h)
                    wide_x[slot, where, t] = move[part]
                    wide_x[slot, where, t, :, :cols] += transported(r, t)[part]
        for slot in range(3):
            put(slot, dot3(wide_x[slot].reshape(tracers * levels, wide), fwd))
        sign = jnp.where(south, -1.0, 1.0).astype(jnp.float32)
        row_p = jnp.where(south, rows - 1, 0)
        lane = lax.broadcasted_iota(jnp.int32, (half_lev, LANE), 1)
        one, cos, sin = (pole[lon, k : k + 1] for k in range(3))
        for t in range(tracers):
            m = north[row_p] * adj[row_p, t] * sign
            for h, target in ((0, keep), (1, send)):
                where = jnp.where(core == 0, h, 1 - h)
                u = wide_x[3, h, t]
                flux[:half_lev, :cols] = jnp.where(where == 0, m[:half_lev], m[half_lev:])
                v = flux[:half_lev]
                c0 = jnp.sum((u + v) * one, axis=1, keepdims=True)
                c1 = jnp.sum((u - v) * cos, axis=1, keepdims=True)
                s1 = jnp.sum((u - v) * sin, axis=1, keepdims=True)
                at = KF % LANE
                lanes = slice(half - LANE, half)
                spot = slice(t * half_lev, (t + 1) * half_lev)
                target[2, spot, lanes] = jnp.where(
                    lane == at, c0, jnp.where(lane == at + 1, c1, jnp.where(lane == at + 2, s1, target[2, spot, lanes]))
                )


def last_kernel(
    lat_count, circle, cutoff, base, recv_a, recv_b, left, right, mine, other, mine_r, other_r, beside_t, beside_o,
    bwd, turn, pole, out, coef,
):
    rows, tracers, levels, cols = out.shape
    half_lev = levels // 2
    half = bwd.shape[1] // 2
    south, polar, beside, even = roles(lat_count)
    lon = lax.axis_index("lon")
    core = lax.rem(lon, 2)

    @pl.when(jnp.logical_not(polar))
    def _():
        row = lax.broadcasted_iota(jnp.int32, (8, LANE), 0)
        lane = lax.broadcasted_iota(jnp.int32, (8, LANE), 1)
        at = (cols - 1) % LANE
        low = jnp.where((row == 1) & (lane == 0), 1.0, 0.0).astype(jnp.float32)
        high = jnp.where((row == 0) & (lane == at), 1.0, 0.0).astype(jnp.float32)
        dims = (((0,), (0,)), ((), ()))
        exact = lax.Precision.HIGHEST
        first = lax.dot_general(left[...], low, dims, precision=exact, preferred_element_type=jnp.float32)
        end = lax.dot_general(right[...], high, dims, precision=exact, preferred_element_type=jnp.float32)
        start = cols // LANE * LANE
        shape = (rows, 2, tracers, half_lev, LANE)
        first, end = first.reshape(shape), end.reshape(shape)
        out[...] = base[...]
        for r in range(rows):
            for h in (0, 1):
                part = slice(h * half_lev, (h + 1) * half_lev)
                out[r, :, part, :LANE] -= first[r, h]
                out[r, :, part, start:] += end[r, h][..., : cols - start]
        row_a = jnp.where(even, rows - 1, 0)
        row_b = rows - 1 - row_a
        sign = jnp.where(even, 1.0, -1.0).astype(jnp.float32)
        out[row_a] += recv_a[...] * sign
        out[row_b] -= recv_b[...] * sign

    @pl.when(polar)
    def _():
        for slot in range(3):
            own, far = mine[slot] + mine_r[slot], other[slot] + other_r[slot]
            if slot == 2:
                own, far = own + beside_t[...], far + beside_o[...]
            coef[slot, core] = own
            coef[slot, 1 - core] = far
        wave = lax.broadcasted_iota(jnp.int32, (1, half), 1)
        a, b = turn[lon, 0:1], turn[lon, 1:2]
        for slot in range(3):
            near = slot + 1
            row = jnp.where(south, rows - 1 - near, near)
            kept = jnp.where(south, cutoff[1, row], cutoff[0, row])
            weight = jnp.where(wave <= kept, jnp.where(wave == 0, 1.0 / circle, 2.0 / circle), 0.0).astype(jnp.float32)
            block = coef[slot].reshape(tracers * levels, 2 * half)
            c, s = block[:, :half], block[:, half:]
            wa, wb = weight * a, weight * b
            back = jnp.concatenate([c * wa + s * wb, s * wa - c * wb], axis=1)
            y = dot3(back, bwd).reshape(2, tracers, half_lev, -1)
            for h in (0, 1):
                out[row, :, h * half_lev : (h + 1) * half_lev, :] = y[h][..., :cols]
        row = jnp.where(south, rows - 1, 0)
        cos, sin = pole[lon, 1:2], pole[lon, 2:3]
        for t in range(tracers):
            for h in (0, 1):
                p = coef[2, h, t * half_lev : (t + 1) * half_lev, half - LANE : half]
                at = KF % LANE
                c0, c1, s1 = p[:, at : at + 1], p[:, at + 1 : at + 2], p[:, at + 2 : at + 3]
                y = (1.0 / circle) * c0 + (2.0 / circle) * (c1 * cos + s1 * sin)
                out[row, t, h * half_lev : (h + 1) * half_lev, :] = y[:, :cols]


def routes(lat_count, lon_count, lats, step):
    return [(a * lon_count + i, a * lon_count + (i ^ step)) for a in lats for i in range(lon_count)]


def fast_body(adj, east, north, cutoff):
    lat_count, lon_count = lax.axis_size("lat"), lax.axis_size("lon")
    rows, tracers, levels, cols = adj.shape
    circle = cols * lon_count
    fwd, bwd, turn, pole = tables(cols, circle, lon_count)
    wide, width = fwd.shape[1:]
    both = ("lat", "lon")
    last = lat_count - 1
    f32 = jnp.float32
    spec = pl.BlockSpec(memory_space=VMEM)
    shape = jax.ShapeDtypeStruct
    share = (3, tracers * levels // 2, width)
    n_rows = rows * tracers * levels
    base, edge_a, edge_b, sides, keep, send = pl.pallas_call(
        functools.partial(local_kernel, lat_count),
        out_shape=[
            shape(adj.shape, f32),
            shape(adj.shape[1:], f32),
            shape(adj.shape[1:], f32),
            shape((8, n_rows), f32),
            shape(share, f32),
            shape(share, f32),
        ],
        in_specs=[spec] * 6,
        out_specs=[spec] * 6,
        scratch_shapes=[VMEM((levels, wide), f32), VMEM((rows, 2, tracers, levels // 2, wide), f32)],
    )(adj, east, north, fwd, turn, pole)

    def move(x, lats, step):
        return lax.ppermute(x, both, routes(lat_count, lon_count, lats, step))

    caps = (0, last)
    nexts = (1, last - 1)
    got = move(send, caps + nexts, 1)
    total = keep + got
    third = total[2]
    third_r = move(third, nexts, 2)
    third_sum = third + third_r
    mine_r = move(total, caps, 2)
    swap_a = [(i ^ 1) for i in range(lat_count)]
    recv_a = lax.ppermute(edge_a, "lat", list(enumerate(swap_a)))
    recv_b = lax.ppermute(edge_b, "lat", [(i, j) for k in range(1, last, 2) for i, j in ((k, k + 1), (k + 1, k))])
    inner = range(1, last)
    ring = [(a * lon_count + i, a * lon_count + (i + 1) % lon_count) for a in inner for i in range(lon_count)]
    left = lax.ppermute(sides, both, ring)
    right = lax.ppermute(sides, both, [(j, i) for i, j in ring])
    other = move(total, caps, 1)
    to_cap = [(a * lon_count + i, b * lon_count + i) for a, b in ((1, 0), (last - 1, last)) for i in range(lon_count)]
    beside_t = lax.ppermute(third_sum, both, to_cap)
    other_r = move(mine_r, caps, 1)
    beside_o = move(beside_t, caps, 1)
    return pl.pallas_call(
        functools.partial(last_kernel, lat_count, circle),
        out_shape=shape(adj.shape, f32),
        in_specs=[pl.BlockSpec(memory_space=pltpu.SMEM)] + [spec] * 14,
        out_specs=spec,
        scratch_shapes=[VMEM((3, 2, tracers * levels // 2, width), f32)],
    )(cutoff, base, recv_a, recv_b, left, right, total, other, mine_r, other_r, beside_t, beside_o, bwd, turn, pole)


full_precision = lax.Precision.HIGHEST


def extended(block, sides, width, periodic):
    for axis, dim in sides:
        count = lax.axis_size(axis)
        forward = [(i, i + 1) for i in range(count - 1)]
        if periodic:
            forward.append((count - 1, 0))
        backward = [(target, source) for source, target in forward]
        low = lax.ppermute(
            lax.slice_in_dim(block, block.shape[dim] - width, None, axis=dim), axis, forward
        )
        high = lax.ppermute(lax.slice_in_dim(block, 0, width, axis=dim), axis, backward)
        block = jnp.concatenate([low, block, high], axis=dim)
    return block


def from_partner(block, axis, stride):
    count = lax.axis_size(axis)
    route = []
    for low in range(count):
        high = low | 1 << stride
        if high != low and high < count:
            route += [(low, high), (high, low)]
    return lax.ppermute(block, axis, route)


def mode_table(columns, modes_kept, circle):
    wavenumber = jnp.arange(modes_kept, dtype=jnp.int32)
    product = columns[:, None] * wavenumber[None, :] % circle
    phases = product.astype(jnp.float32) * (2.0 * math.pi / circle)
    return jnp.concatenate([jnp.cos(phases), jnp.sin(phases)], axis=1)


def spectral_weights(latitude, cutoff, modes_kept, circle, total_lat):
    cap_lat = cutoff.shape[1]
    offsets = jnp.arange(cap_lat, dtype=jnp.int32)
    north_hit = latitude[..., None] == offsets
    south_hit = latitude[..., None] == total_lat - cap_lat + offsets
    chosen = jnp.sum(
        jnp.where(north_hit, cutoff[0], 0) + jnp.where(south_hit, cutoff[1], 0), axis=-1
    )
    wavenumber = jnp.arange(2 * modes_kept, dtype=jnp.int32) % modes_kept
    mode_weight = jnp.where(wavenumber == 0, 1.0, 2.0) / circle
    kept_mask = wavenumber <= chosen[..., None]
    return jnp.where(kept_mask, mode_weight, 0.0).astype(jnp.float32)


def general_body(adj_next, east_courant, north_courant, cutoff):
    lat_count = lax.axis_size("lat")
    lon_count = lax.axis_size("lon")
    lat_index = lax.axis_index("lat")
    lon_index = lax.axis_index("lon")
    lat_rows, tracers, levels, lon_cols = adj_next.shape
    circle = lon_cols * lon_count
    total_lat = lat_rows * lat_count
    modes_kept = KF
    cap_lat = cutoff.shape[1]
    zonal_flux = east_courant[:, None] * adj_next
    meridional = north_courant[:, None] * adj_next
    lon_padded = extended(zonal_flux, (("lon", 3),), 1, True)
    result = adj_next + lon_padded[..., 2:] - lon_padded[..., :-2]
    lat_padded = extended(meridional, (("lat", 0),), 1, False)
    result = result + lat_padded[2:] - lat_padded[:-2]
    edge_row = jnp.where(lat_index == 0, meridional[0], meridional[-1])
    pole_bit = lon_count.bit_length() - 2
    partner = from_partner(edge_row, "lon", pole_bit)
    north_sign = jnp.where(lat_index == 0, 1.0, 0.0).astype(jnp.float32)
    south_sign = jnp.where(lat_index == lat_count - 1, -1.0, 0.0).astype(jnp.float32)
    result = result.at[0].add(north_sign * partner)
    result = result.at[-1].add(south_sign * partner)
    latitude = lat_index * lat_rows + jnp.arange(lat_rows, dtype=jnp.int32)
    in_cap = (latitude < cap_lat) | (latitude >= total_lat - cap_lat)
    local_cols = lon_index * lon_cols + jnp.arange(lon_cols, dtype=jnp.int32)
    local_table = mode_table(local_cols, modes_kept, circle)
    weights = spectral_weights(latitude, cutoff, modes_kept, circle, total_lat)
    partial_sum = jnp.einsum(
        "acvn,nk->acvk",
        result,
        local_table,
        precision=full_precision,
        preferred_element_type=jnp.float32,
    )
    level_share = lax.psum_scatter(partial_sum, "lon", scatter_dimension=2, tiled=True)
    level_share = level_share * weights[:, None, None, :]
    totals = lax.all_gather(level_share, "lon", axis=2, tiled=True)
    rebuilt = jnp.einsum(
        "acvk,nk->acvn",
        totals,
        local_table,
        precision=full_precision,
        preferred_element_type=jnp.float32,
    )
    output = jnp.where(in_cap[:, None, None, None], rebuilt, result)
    return output


def body(adj, east, north, cutoff):
    lat_count, lon_count = lax.axis_size("lat"), lax.axis_size("lon")
    one_band = cutoff.shape[1] == adj.shape[0] == 4
    if one_band and lon_count == 4 and lat_count % 2 == 0 and lat_count >= 4 and adj.shape[2] % 16 == 0:
        return fast_body(adj, east, north, cutoff)
    return general_body(adj, east, north, cutoff)


def solution(mesh):
    return jax.shard_map(
        body,
        mesh=mesh,
        in_specs=(P("lat", None, None, "lon"), P("lat", None, "lon"), P("lat", None, "lon"), P()),
        out_specs=P("lat", None, None, "lon"),
        check_vma=False,
    )
```

```python
import functools
import math

import jax
import jax.numpy as jnp
import ml_dtypes
import numpy as np
from jax import lax
from jax.experimental import pallas as pl
from jax.experimental.pallas import tpu as pltpu
from jax.sharding import PartitionSpec as P

KF = 352
LANE = 128
VMEM = pltpu.VMEM
OUT = pltpu.VMEM
PLAIN_COST = pl.CostEstimate(flops=0, bytes_accessed=40_000_000, transcendentals=0)


def ceil_to(value, unit):
    return -(-value // unit) * unit


def split16(table):
    high = table.astype(ml_dtypes.bfloat16)
    low = (table - high.astype(np.float64)).astype(ml_dtypes.bfloat16)
    return np.stack([high, low])


def tables(cols, circle, lon_count):
    wide = ceil_to(cols + 2, LANE)
    half = ceil_to(KF + 2, LANE)
    place = np.zeros(wide, np.int64)
    place[: cols + 1] = np.arange(cols + 1)
    place[-1] = -1
    live = np.zeros(wide)
    live[: cols + 1] = 1
    live[-1] = 1
    mode = np.arange(KF)
    phase = 2 * np.pi * ((place[:, None] * mode[None]) % circle) / circle
    forward = np.zeros((wide, 2 * half))
    forward[:, :KF] = np.cos(phase) * live[:, None]
    forward[:, half : half + KF] = np.sin(phase) * live[:, None]
    backward = forward.T.copy()
    backward[:, cols:] = 0
    turn = np.zeros((lon_count, 2, half), np.float32)
    angle = 2 * np.pi * ((np.arange(lon_count)[:, None] * mode[None]) % lon_count) / lon_count
    turn[:, 0, :KF] = np.cos(angle)
    turn[:, 1, :KF] = np.sin(angle)
    pole = np.zeros((lon_count, 4, wide), np.float32)
    for index in range(lon_count):
        first = 2 * np.pi * (place + index * cols) / circle
        pole[index, 0] = live
        pole[index, 1] = np.cos(first) * live
        pole[index, 2] = np.sin(first) * live
    return split16(forward), split16(backward), turn, pole


def dot3(block, table_ref):
    high = block.astype(jnp.bfloat16)
    low = (block - high.astype(jnp.float32)).astype(jnp.bfloat16)
    total = jnp.dot(high, table_ref[0], preferred_element_type=jnp.float32)
    total += jnp.dot(high, table_ref[1], preferred_element_type=jnp.float32)
    return total + jnp.dot(low, table_ref[0], preferred_element_type=jnp.float32)


def roles(lat_count):
    lat = lax.axis_index("lat")
    last = lat_count - 1
    north, south = lat == 0, lat == last
    polar = jnp.logical_or(north, south)
    beside = jnp.logical_or(lat == 1, lat == last - 1)
    even = lax.rem(lat, 2) == 0
    return south, polar, beside, even


def local_kernel(
    lat_count, adj_hbm, east_hbm, north_hbm, fwd_hbm, turn_hbm, pole_hbm, base, edge_a, edge_b, sides, keep, send,
    adj, east, north, fwd, turn, pole, flux, wide_x, ends, sems,
):
    rows, tracers, levels, cols = adj.shape
    wide = flux.shape[-1]
    south, polar, beside, even = roles(lat_count)
    lon = lax.axis_index("lon")
    core = lax.rem(lon, 2)
    half_lev = levels // 2
    half = fwd.shape[-1] // 2
    fetch = [
        pltpu.make_async_copy(source, target, sems.at[n])
        for n, (source, target) in enumerate(
            ((adj_hbm, adj), (east_hbm, east), (north_hbm, north), (turn_hbm, turn), (pole_hbm, pole), (fwd_hbm, fwd))
        )
    ]
    for copy in fetch:
        copy.start()
    for copy in fetch[:3]:
        copy.wait()
    row_a = jnp.where(even, rows - 1, 0)
    row_b = rows - 1 - row_a
    edge_a[...] = north[row_a][None] * adj[row_a]
    edge_b[...] = north[row_b][None] * adj[row_b]
    flux[:, cols:] = jnp.zeros((levels, wide - cols), jnp.float32)

    def transported(r, t):
        out = adj[r, t]
        if r + 1 < rows:
            out = out + north[r + 1] * adj[r + 1, t]
        if r > 0:
            out = out - north[r - 1] * adj[r - 1, t]
        return out

    def spread(r, t):
        flux[:, :cols] = east[r] * adj[r, t]
        f = flux[...]
        return pltpu.roll(f, wide - 1, 1) - pltpu.roll(f, 1, 1), f

    def put(slot, p):
        a, b = turn[lon, 0:1], turn[lon, 1:2]
        c, s = p[:, :half], p[:, half:]
        c, s = c * a - s * b, s * a + c * b
        n = c.shape[0] // 2
        keep[slot, :, :half] = c[:n]
        keep[slot, :, half:] = s[:n]
        send[slot, :, :half] = c[n:]
        send[slot, :, half:] = s[n:]

    @pl.when(jnp.logical_not(polar))
    def _():
        start = cols // LANE * LANE
        lane = lax.broadcasted_iota(jnp.int32, (levels, LANE), 1)
        at = cols - 1 - start
        for r in range(rows):
            for t in range(tracers):
                move, f = spread(r, t)
                base[r, t] = transported(r, t) + move[:, :cols]
                ends[r, t] = jnp.where(lane == 0, f[:, :LANE], jnp.where(lane == at, f[:, start : start + LANE], 0.0))
        row = lax.broadcasted_iota(jnp.int32, (8, LANE), 0)
        lane = lax.broadcasted_iota(jnp.int32, (8, LANE), 1)
        pick = jnp.where((row == 0) & (lane == 0) | (row == 1) & (lane == at), 1.0, 0.0).astype(jnp.float32)
        sides[...] = lax.dot_general(
            pick,
            ends[...].reshape(rows * tracers * levels, LANE),
            (((1,), (1,)), ((), ())),
            precision=lax.Precision.HIGHEST,
            preferred_element_type=jnp.float32,
        )

    @pl.when(beside)
    def _():
        sign = jnp.where(even, -1.0, 1.0).astype(jnp.float32)
        wide_x[2] = jnp.zeros(wide_x.shape[1:], jnp.float32)
        for t in range(tracers):
            m = edge_a[t] * sign
            wide_x[2, core, t, :, :cols] = m[:half_lev]
            wide_x[2, 1 - core, t, :, :cols] = m[half_lev:]

    @pl.when(polar)
    def _():
        for r in range(rows):
            near = jnp.where(south, rows - 1 - r, r)
            slot = lax.rem(near + rows - 1, rows)
            for t in range(tracers):
                move, _ = spread(r, t)
                for h in (0, 1):
                    part = slice(h * half_lev, (h + 1) * half_lev)
                    where = jnp.where(core == 0, h, 1 - h)
                    wide_x[slot, where, t] = move[part]
                    wide_x[slot, where, t, :, :cols] += transported(r, t)[part]

    for copy in fetch[3:]:
        copy.wait()

    @pl.when(beside)
    def _():
        put(2, dot3(wide_x[2].reshape(tracers * levels, wide), fwd))

    @pl.when(polar)
    def _():
        for slot in range(3):
            put(slot, dot3(wide_x[slot].reshape(tracers * levels, wide), fwd))
        sign = jnp.where(south, -1.0, 1.0).astype(jnp.float32)
        row_p = jnp.where(south, rows - 1, 0)
        lane = lax.broadcasted_iota(jnp.int32, (half_lev, LANE), 1)
        one, cos, sin = (pole[lon, k : k + 1] for k in range(3))
        for t in range(tracers):
            m = north[row_p] * adj[row_p, t] * sign
            for h, target in ((0, keep), (1, send)):
                where = jnp.where(core == 0, h, 1 - h)
                u = wide_x[3, h, t]
                flux[:half_lev, :cols] = jnp.where(where == 0, m[:half_lev], m[half_lev:])
                v = flux[:half_lev]
                c0 = jnp.sum((u + v) * one, axis=1, keepdims=True)
                c1 = jnp.sum((u - v) * cos, axis=1, keepdims=True)
                s1 = jnp.sum((u - v) * sin, axis=1, keepdims=True)
                at = KF % LANE
                lanes = slice(half - LANE, half)
                spot = slice(t * half_lev, (t + 1) * half_lev)
                target[2, spot, lanes] = jnp.where(
                    lane == at, c0, jnp.where(lane == at + 1, c1, jnp.where(lane == at + 2, s1, target[2, spot, lanes]))
                )


def sum_kernel(x, y, out, third):
    out[...] = x[...] + y[...]
    third[...] = out[2]


def total_kernel(lat_count, plain, mine, across, beside, beside_across, out):
    _, polar, _, _ = roles(lat_count)

    @pl.when(polar)
    def _():
        out[...] = mine[...] + across[...]
        out[2] += beside[...] + beside_across[...]


def plain_kernel(lat_count, base, recv_a, recv_b, left, right, beside, beside_across, out, rows_ref, sems):
    rows, tracers, levels, cols = base.shape
    south, polar, _, even = roles(lat_count)

    @pl.when(jnp.logical_not(polar))
    def _():
        row = lax.broadcasted_iota(jnp.int32, (8, LANE), 0)
        lane = lax.broadcasted_iota(jnp.int32, (8, LANE), 1)
        start = cols // LANE * LANE
        low = jnp.where((row == 1) & (lane == 0), 1.0, 0.0).astype(jnp.float32)
        high = jnp.where((row == 0) & (lane == cols - 1 - start), 1.0, 0.0).astype(jnp.float32)
        dims = (((0,), (0,)), ((), ()))
        exact = lax.Precision.HIGHEST
        first = lax.dot_general(left[...], low, dims, precision=exact, preferred_element_type=jnp.float32)
        end = lax.dot_general(right[...], high, dims, precision=exact, preferred_element_type=jnp.float32)
        shape = (rows, tracers, levels, LANE)
        first, end = first.reshape(shape), end.reshape(shape)
        up_a = jnp.where(even, 1.0, 0.0).astype(jnp.float32)
        copies = []
        for r in range(rows):
            value = base[r]
            if r == rows - 1:
                value = value + jnp.where(even, recv_a[...], recv_b[...])
            if r == 0:
                value = value - jnp.where(even, recv_b[...], recv_a[...])
            rows_ref[r] = value
            rows_ref[r, :, :, :LANE] -= first[r]
            rows_ref[r, :, :, start:] += end[r][..., : cols - start]
            copies.append(pltpu.make_async_copy(rows_ref.at[r], out.at[r], sems.at[r]))
            copies[-1].start()
        for copy in copies:
            copy.wait()


def cap_kernel(lat_count, circle, cutoff, given, mine, other, bwd, turn, pole, out, coef, rows_ref, sems):
    rows, tracers, levels, cols = out.shape
    half_lev = levels // 2
    half = bwd.shape[1] // 2
    south, polar, _, _ = roles(lat_count)
    lon = lax.axis_index("lon")
    core = lax.rem(lon, 2)

    @pl.when(polar)
    def _():
        copies = []

        def leave(k, row):
            copies.append(pltpu.make_async_copy(rows_ref.at[k], out.at[row], sems.at[k]))
            copies[-1].start()

        coef[core] = mine[...]
        coef[1 - core] = other[...]
        cos, sin = pole[lon, 1:2], pole[lon, 2:3]
        at = KF % LANE
        for t in range(tracers):
            for h in (0, 1):
                p = coef[h, 2, t * half_lev : (t + 1) * half_lev, half - LANE : half]
                c0, c1, s1 = p[:, at : at + 1], p[:, at + 1 : at + 2], p[:, at + 2 : at + 3]
                y = (1.0 / circle) * c0 + (2.0 / circle) * (c1 * cos + s1 * sin)
                rows_ref[3, t, h * half_lev : (h + 1) * half_lev, :] = y[:, :cols]
        leave(3, jnp.where(south, rows - 1, 0))
        wave = lax.broadcasted_iota(jnp.int32, (1, half), 1)
        a, b = turn[lon, 0:1], turn[lon, 1:2]
        for slot in range(3):
            near = slot + 1
            row = jnp.where(south, rows - 1 - near, near)
            kept = jnp.where(south, cutoff[1, row], cutoff[0, row])
            weight = jnp.where(wave <= kept, jnp.where(wave == 0, 1.0 / circle, 2.0 / circle), 0.0).astype(jnp.float32)
            block = coef[:, slot].reshape(tracers * levels, 2 * half)
            c, s = block[:, :half], block[:, half:]
            wa, wb = weight * a, weight * b
            back = jnp.concatenate([c * wa + s * wb, s * wa - c * wb], axis=1)
            y = dot3(back, bwd).reshape(2, tracers, half_lev, -1)
            for h in (0, 1):
                rows_ref[slot, :, h * half_lev : (h + 1) * half_lev, :] = y[h][..., :cols]
            leave(slot, row)
        for copy in copies:
            copy.wait()


def fast_body(adj, east, north, cutoff):
    lat_count, lon_count = lax.axis_size("lat"), lax.axis_size("lon")
    rows, tracers, levels, cols = adj.shape
    circle = cols * lon_count
    fwd, bwd, turn, pole = tables(cols, circle, lon_count)
    wide, width = fwd.shape[1:]
    both = ("lat", "lon")
    last = lat_count - 1
    f32, bf16 = jnp.float32, jnp.bfloat16
    vmem = pl.BlockSpec(memory_space=VMEM)
    anywhere = pl.BlockSpec(memory_space=pl.ANY)
    far = pl.BlockSpec(memory_space=pltpu.HBM)
    params = pltpu.CompilerParams(vmem_limit_bytes=40 << 20)
    dma = pltpu.SemaphoreType.DMA
    share = (3, tracers * levels // 2, width)
    n_rows = rows * tracers * levels

    def near(x):
        return pltpu.with_memory_space_constraint(x, VMEM)

    def hbm(x):
        return pltpu.with_memory_space_constraint(x, pltpu.HBM)

    base, edge_a, edge_b, sides, keep, send = pl.pallas_call(
        functools.partial(local_kernel, lat_count),
        out_shape=[
            OUT(adj.shape, f32),
            OUT(adj.shape[1:], f32),
            OUT(adj.shape[1:], f32),
            OUT((8, n_rows), f32),
            OUT(share, f32),
            OUT(share, f32),
        ],
        in_specs=[far] * 6,
        out_specs=[vmem] * 6,
        scratch_shapes=[
            VMEM(adj.shape, f32),
            VMEM(east.shape, f32),
            VMEM(north.shape, f32),
            VMEM(fwd.shape, bf16),
            VMEM(turn.shape, f32),
            VMEM(pole.shape, f32),
            VMEM((levels, wide), f32),
            VMEM((rows, 2, tracers, levels // 2, wide), f32),
            VMEM((rows, tracers, levels, LANE), f32),
            dma((6,)),
        ],
        compiler_params=params,
    )(*map(hbm, (adj, east, north, fwd, turn, pole)))

    def hop(x, pairs):
        return lax.ppermute(x, both, [(a * lon_count + i, b * lon_count + j) for a, i, b, j in pairs])

    lons = range(lon_count)
    caps = (0, last)
    to_cap = ((1, 0), (last - 1, last))
    got = hop(send, [(a, i, a, i ^ 1) for a in (0, 1, last - 1, last) for i in lons])
    edge_pairs = [(i, i ^ 1) for i in range(lat_count) if (i, i ^ 1) not in to_cap]
    recv_a = lax.ppermute(edge_a, "lat", edge_pairs)
    total, third = pl.pallas_call(
        sum_kernel,
        out_shape=[OUT(share, f32), OUT(share[1:], f32)],
        in_specs=[vmem] * 2,
        out_specs=[vmem] * 2,
        compiler_params=params,
    )(near(keep), near(got))
    across = hop(total, [(a, i, a, i ^ 2) for a in caps for i in lons])
    beside = hop(third, [(a, i, b, i) for a, b in to_cap for i in lons])
    beside_across = hop(third, [(a, i, b, i ^ 2) for a, b in to_cap for i in lons])
    recv_b = lax.ppermute(edge_b, "lat", [(i, j) for k in range(1, last, 2) for i, j in ((k, k + 1), (k + 1, k))])
    ring = [(a, i, a, (i + 1) % lon_count) for a in range(1, last) for i in lons]
    left = hop(sides, ring)
    right = hop(sides, [(a, j, a, i) for a, i, _, j in ring])
    plain = pl.pallas_call(
        functools.partial(plain_kernel, lat_count),
        out_shape=jax.ShapeDtypeStruct(adj.shape, f32),
        in_specs=[vmem] * 7,
        out_specs=anywhere,
        scratch_shapes=[VMEM(adj.shape, f32), dma((rows,))],
        compiler_params=params,
        cost_estimate=PLAIN_COST,
    )(near(base), near(recv_a), near(recv_b), near(left), near(right), near(beside), near(beside_across))
    mine = pl.pallas_call(
        functools.partial(total_kernel, lat_count),
        out_shape=OUT(share, f32),
        in_specs=[far] + [vmem] * 4,
        out_specs=vmem,
        compiler_params=params,
    )(hbm(plain), near(total), near(across), near(beside), near(beside_across))
    other = hop(mine, [(a, i, a, i ^ 1) for a in caps for i in lons])
    return pl.pallas_call(
        functools.partial(cap_kernel, lat_count, circle),
        out_shape=jax.ShapeDtypeStruct(adj.shape, f32),
        in_specs=[pl.BlockSpec(memory_space=pltpu.SMEM), anywhere] + [vmem] * 5,
        out_specs=anywhere,
        scratch_shapes=[
            VMEM((2,) + share, f32),
            VMEM(adj.shape, f32),
            dma((rows,)),
        ],
        input_output_aliases={1: 0},
        compiler_params=params,
    )(cutoff, plain, near(mine), near(other), near(bwd), near(turn), near(pole))


full_precision = lax.Precision.HIGHEST


def extended(block, sides, width, periodic):
    for axis, dim in sides:
        count = lax.axis_size(axis)
        forward = [(i, i + 1) for i in range(count - 1)]
        if periodic:
            forward.append((count - 1, 0))
        backward = [(target, source) for source, target in forward]
        low = lax.ppermute(
            lax.slice_in_dim(block, block.shape[dim] - width, None, axis=dim), axis, forward
        )
        high = lax.ppermute(lax.slice_in_dim(block, 0, width, axis=dim), axis, backward)
        block = jnp.concatenate([low, block, high], axis=dim)
    return block


def from_partner(block, axis, stride):
    count = lax.axis_size(axis)
    route = []
    for low in range(count):
        high = low | 1 << stride
        if high != low and high < count:
            route += [(low, high), (high, low)]
    return lax.ppermute(block, axis, route)


def mode_table(columns, modes_kept, circle):
    wavenumber = jnp.arange(modes_kept, dtype=jnp.int32)
    product = columns[:, None] * wavenumber[None, :] % circle
    phases = product.astype(jnp.float32) * (2.0 * math.pi / circle)
    return jnp.concatenate([jnp.cos(phases), jnp.sin(phases)], axis=1)


def spectral_weights(latitude, cutoff, modes_kept, circle, total_lat):
    cap_lat = cutoff.shape[1]
    offsets = jnp.arange(cap_lat, dtype=jnp.int32)
    north_hit = latitude[..., None] == offsets
    south_hit = latitude[..., None] == total_lat - cap_lat + offsets
    chosen = jnp.sum(
        jnp.where(north_hit, cutoff[0], 0) + jnp.where(south_hit, cutoff[1], 0), axis=-1
    )
    wavenumber = jnp.arange(2 * modes_kept, dtype=jnp.int32) % modes_kept
    mode_weight = jnp.where(wavenumber == 0, 1.0, 2.0) / circle
    kept_mask = wavenumber <= chosen[..., None]
    return jnp.where(kept_mask, mode_weight, 0.0).astype(jnp.float32)


def general_body(adj_next, east_courant, north_courant, cutoff):
    lat_count = lax.axis_size("lat")
    lon_count = lax.axis_size("lon")
    lat_index = lax.axis_index("lat")
    lon_index = lax.axis_index("lon")
    lat_rows, tracers, levels, lon_cols = adj_next.shape
    circle = lon_cols * lon_count
    total_lat = lat_rows * lat_count
    modes_kept = KF
    cap_lat = cutoff.shape[1]
    zonal_flux = east_courant[:, None] * adj_next
    meridional = north_courant[:, None] * adj_next
    lon_padded = extended(zonal_flux, (("lon", 3),), 1, True)
    result = adj_next + lon_padded[..., 2:] - lon_padded[..., :-2]
    lat_padded = extended(meridional, (("lat", 0),), 1, False)
    result = result + lat_padded[2:] - lat_padded[:-2]
    edge_row = jnp.where(lat_index == 0, meridional[0], meridional[-1])
    pole_bit = lon_count.bit_length() - 2
    partner = from_partner(edge_row, "lon", pole_bit)
    north_sign = jnp.where(lat_index == 0, 1.0, 0.0).astype(jnp.float32)
    south_sign = jnp.where(lat_index == lat_count - 1, -1.0, 0.0).astype(jnp.float32)
    result = result.at[0].add(north_sign * partner)
    result = result.at[-1].add(south_sign * partner)
    latitude = lat_index * lat_rows + jnp.arange(lat_rows, dtype=jnp.int32)
    in_cap = (latitude < cap_lat) | (latitude >= total_lat - cap_lat)
    local_cols = lon_index * lon_cols + jnp.arange(lon_cols, dtype=jnp.int32)
    local_table = mode_table(local_cols, modes_kept, circle)
    weights = spectral_weights(latitude, cutoff, modes_kept, circle, total_lat)
    partial_sum = jnp.einsum(
        "acvn,nk->acvk",
        result,
        local_table,
        precision=full_precision,
        preferred_element_type=jnp.float32,
    )
    level_share = lax.psum_scatter(partial_sum, "lon", scatter_dimension=2, tiled=True)
    level_share = level_share * weights[:, None, None, :]
    totals = lax.all_gather(level_share, "lon", axis=2, tiled=True)
    rebuilt = jnp.einsum(
        "acvk,nk->acvn",
        totals,
        local_table,
        precision=full_precision,
        preferred_element_type=jnp.float32,
    )
    output = jnp.where(in_cap[:, None, None, None], rebuilt, result)
    return output


def body(adj, east, north, cutoff):
    lat_count, lon_count = lax.axis_size("lat"), lax.axis_size("lon")
    one_band = cutoff.shape[1] == adj.shape[0] == 4
    if one_band and lon_count == 4 and lat_count % 2 == 0 and lat_count >= 4 and adj.shape[2] % 16 == 0:
        return fast_body(adj, east, north, cutoff)
    return general_body(adj, east, north, cutoff)


def solution(mesh):
    return jax.shard_map(
        body,
        mesh=mesh,
        in_specs=(P("lat", None, None, "lon"), P("lat", None, "lon"), P("lat", None, "lon"), P()),
        out_specs=P("lat", None, None, "lon"),
        check_vma=False,
    )
```

```python
import functools
import math

import jax
import jax.numpy as jnp
import ml_dtypes
import numpy as np
from jax import lax
from jax.experimental import pallas as pl
from jax.experimental.pallas import tpu as pltpu
from jax.sharding import PartitionSpec as P

KF = 352
LANE = 128
VMEM = pltpu.VMEM
HBM = pltpu.HBM
HEAVY = pl.CostEstimate(flops=2**37, bytes_accessed=0, transcendentals=0)
LIGHT = pl.CostEstimate(flops=0, bytes_accessed=1000, transcendentals=0)


def ceil_to(value, unit):
    return -(-value // unit) * unit


def split16(table):
    high = table.astype(ml_dtypes.bfloat16)
    low = (table - high.astype(np.float64)).astype(ml_dtypes.bfloat16)
    return np.stack([high, low])


def tables(cols, circle, lon_count):
    wide = ceil_to(cols + 2, LANE)
    half = ceil_to(KF + 2, LANE)
    place = np.zeros(wide, np.int64)
    place[: cols + 1] = np.arange(cols + 1)
    place[-1] = -1
    live = np.zeros(wide)
    live[: cols + 1] = 1
    live[-1] = 1
    mode = np.arange(KF)
    phase = 2 * np.pi * ((place[:, None] * mode[None]) % circle) / circle
    forward = np.zeros((wide, 2 * half))
    forward[:, :KF] = np.cos(phase) * live[:, None]
    forward[:, half : half + KF] = np.sin(phase) * live[:, None]
    backward = forward.T.copy()
    backward[:, cols:] = 0
    turn = np.zeros((lon_count, 2, half), np.float32)
    angle = 2 * np.pi * ((np.arange(lon_count)[:, None] * mode[None]) % lon_count) / lon_count
    turn[:, 0, :KF] = np.cos(angle)
    turn[:, 1, :KF] = np.sin(angle)
    pole = np.zeros((lon_count, 4, wide), np.float32)
    for index in range(lon_count):
        first = 2 * np.pi * (place + index * cols) / circle
        pole[index, 0] = live
        pole[index, 1] = np.cos(first) * live
        pole[index, 2] = np.sin(first) * live
    return split16(forward), split16(backward), turn, pole


def dot3(block, table_ref):
    rows = block.shape[0]
    high = block.astype(jnp.bfloat16)
    low = (block - high.astype(jnp.float32)).astype(jnp.bfloat16)
    stack = jnp.dot(jnp.concatenate([high, low]), table_ref[0], preferred_element_type=jnp.float32)
    return stack[:rows] + stack[rows:] + jnp.dot(high, table_ref[1], preferred_element_type=jnp.float32)


def latitude_role(lat_count):
    lat = lax.axis_index("lat")
    south = lat == lat_count - 1
    return south, jnp.logical_or(lat == 0, south), lax.rem(lat, 2) == 0


def longitude_role():
    lon = lax.axis_index("lon")
    core = lax.rem(lon, 2)
    return lon, core, core == 0


def turned(p, turn, lon):
    half = p.shape[1] // 2
    a, b = turn[lon, 0:1], turn[lon, 1:2]
    c, s = p[:, :half], p[:, half:]
    return c * a - s * b, s * a + c * b


def weighted(block, kept, circle, turn, lon):
    half = block.shape[1] // 2
    wave = lax.broadcasted_iota(jnp.int32, (1, half), 1)
    weight = jnp.where(wave <= kept, jnp.where(wave == 0, 1.0 / circle, 2.0 / circle), 0.0).astype(jnp.float32)
    wa, wb = weight * turn[lon, 0:1], weight * turn[lon, 1:2]
    c, s = block[:, :half], block[:, half:]
    return jnp.concatenate([c * wa + s * wb, s * wa - c * wb], axis=1)


def edge_kernel(lat_count, adj_hbm, north_hbm, edge, adj, north, sems):
    _, _, even = latitude_role(lat_count)
    row = jnp.where(even, adj_hbm.shape[0] - 1, 0)
    copies = (
        pltpu.make_async_copy(adj_hbm.at[row], adj, sems.at[0]),
        pltpu.make_async_copy(north_hbm.at[row], north, sems.at[1]),
    )
    for copy in copies:
        copy.start()
    for copy in copies:
        copy.wait()
    edge[...] = north[...][None] * adj[...]


def local_kernel(
    lat_count, after, adj_hbm, east_hbm, north_hbm, fwd_hbm, turn_hbm, pole_hbm, base, keep, send, third, fwd, turn,
    adj, east, north, pole, flux, wide_x, ends, sems,
):
    fetch = [
        pltpu.make_async_copy(source, target, sems.at[n])
        for n, (source, target) in enumerate(
            ((adj_hbm, adj), (east_hbm, east), (north_hbm, north), (turn_hbm, turn), (pole_hbm, pole), (fwd_hbm, fwd))
        )
    ]
    for copy in fetch:
        copy.start()
    for copy in fetch[:3]:
        copy.wait()
    rows, tracers, levels, cols = adj.shape
    wide = flux.shape[-1]
    south, polar, even = latitude_role(lat_count)
    lon, own, _ = longitude_role()
    half_lev = levels // 2
    n_half = tracers * half_lev
    half = fwd.shape[-1] // 2
    row_b = jnp.where(even, 0, rows - 1)
    flux[:, cols:] = jnp.zeros((levels, wide - cols), jnp.float32)

    def transported(r, t):
        out = adj[r, t]
        if r + 1 < rows:
            out = out + north[r + 1] * adj[r + 1, t]
        if r > 0:
            out = out - north[r - 1] * adj[r - 1, t]
        return out

    def spread(r, t):
        flux[:, :cols] = east[r] * adj[r, t]
        f = flux[...]
        return pltpu.roll(f, wide - 1, 1) - pltpu.roll(f, 1, 1), f

    @pl.when(jnp.logical_not(polar))
    def _():
        start = cols // LANE * LANE
        lane = lax.broadcasted_iota(jnp.int32, (levels, LANE), 1)
        at = cols - 1 - start
        for r in range(rows):
            for t in range(tracers):
                move, f = spread(r, t)
                base[r, t] = transported(r, t) + move[:, :cols]
                ends[r, t] = jnp.where(lane == 0, f[:, :LANE], jnp.where(lane == at, f[:, start : start + LANE], 0.0))
        row = lax.broadcasted_iota(jnp.int32, (8, LANE), 0)
        lane = lax.broadcasted_iota(jnp.int32, (8, LANE), 1)
        pick = jnp.where((row == 0) & (lane == 0) | (row == 1) & (lane == at), 1.0, 0.0).astype(jnp.float32)
        sides = lax.dot_general(
            pick,
            ends[...].reshape(rows * tracers * levels, LANE),
            (((1,), (1,)), ((), ())),
            precision=lax.Precision.HIGHEST,
            preferred_element_type=jnp.float32,
        )
        send[:8, : sides.shape[1]] = sides
        for t in range(tracers):
            keep[t * levels : (t + 1) * levels, :cols] = north[row_b] * adj[row_b, t]
        for copy in fetch[3:]:
            copy.wait()

    @pl.when(polar)
    def _():
        for r in range(rows):
            near = jnp.where(south, rows - 1 - r, r)
            slot = lax.rem(near + rows - 1, rows)
            for t in range(tracers):
                move, _ = spread(r, t)
                for h in (0, 1):
                    part = slice(h * half_lev, (h + 1) * half_lev)
                    where = jnp.where(own == h, 0, 1)
                    wide_x[slot, where, t] = move[part]
                    wide_x[slot, where, t, :, :cols] += transported(r, t)[part]
        for copy in fetch[3:]:
            copy.wait()
        c, s = turned(dot3(wide_x[:2].reshape(4 * n_half, wide), fwd), turn, lon)
        for slot in range(2):
            spot = slice(slot * n_half, (slot + 1) * n_half)
            first = slice(2 * slot * n_half, (2 * slot + 1) * n_half)
            second = slice((2 * slot + 1) * n_half, (2 * slot + 2) * n_half)
            keep[spot, :half], keep[spot, half:] = c[first], s[first]
            send[spot, :half], send[spot, half:] = c[second], s[second]
        third[...] = wide_x[2].reshape(tracers * levels, wide)
        sign = jnp.where(south, -1.0, 1.0).astype(jnp.float32)
        row_p = jnp.where(south, rows - 1, 0)
        lane = lax.broadcasted_iota(jnp.int32, (half_lev, LANE), 1)
        one, cos, sin = (pole[lon, k : k + 1] for k in range(3))
        for t in range(tracers):
            m = north[row_p] * adj[row_p, t] * sign
            for k, target in ((0, keep), (1, send)):
                u = wide_x[3, k, t]
                flux[:half_lev, :cols] = jnp.where(own == k, m[:half_lev], m[half_lev:])
                v = flux[:half_lev]
                c0 = jnp.sum((u + v) * one, axis=1, keepdims=True)
                c1 = jnp.sum((u - v) * cos, axis=1, keepdims=True)
                s1 = jnp.sum((u - v) * sin, axis=1, keepdims=True)
                at = KF % LANE
                lanes = slice(half - LANE, half)
                spot = slice(t * half_lev, (t + 1) * half_lev)
                target[spot, lanes] = jnp.where(
                    lane == at, c0, jnp.where(lane == at + 1, c1, jnp.where(lane == at + 2, s1, target[spot, lanes]))
                )


def third_kernel(lat_count, local, recv, passed, after, fwd, turn, keep, send, block):
    tracers, levels, cols = recv.shape
    south, polar, _ = latitude_role(lat_count)
    lon, own, _ = longitude_role()
    half_lev = levels // 2
    n_half = tracers * half_lev
    half = fwd.shape[-1] // 2

    @pl.when(jnp.logical_not(polar))
    def _():
        keep[:8] = passed[:8]

    @pl.when(polar)
    def _():
        sign = jnp.where(south, -1.0, 1.0).astype(jnp.float32)
        block[...] = local[...]
        for t in range(tracers):
            m = recv[t] * sign
            for k in (0, 1):
                first = k * n_half + t * half_lev
                block[first : first + half_lev, :cols] += jnp.where(own == k, m[:half_lev], m[half_lev:])
        c, s = turned(dot3(block[...], fwd), turn, lon)
        keep[:, :half], keep[:, half:] = c[:n_half], s[:n_half]
        send[:, :half], send[:, half:] = c[n_half:], s[n_half:]


def token_kernel(x, *rest):
    rest[-1][...] = x[:8, :LANE]


def sum_kernel(lat_count, mine, got, after, out):
    _, polar, _ = latitude_role(lat_count)

    @pl.when(polar)
    def _():
        out[...] = mine[...] + got[...]

    @pl.when(jnp.logical_not(polar))
    def _():
        out[...] = mine[...]


def total_kernel(lat_count, mine, across, third, third_across, after, out):
    _, polar, _ = latitude_role(lat_count)
    count = mine.shape[0]

    @pl.when(polar)
    def _():
        out[:count] = mine[...] + across[...]
        out[count:] = third[...] + third_across[...]


def place(rows_ref, k, y, cols, half_lev):
    y = y.reshape(2, -1, half_lev, y.shape[-1])
    for h in (0, 1):
        rows_ref[k, :, h * half_lev : (h + 1) * half_lev, :] = y[h][..., :cols]


def finish_kernel(
    lat_count, circle, cutoff, base, recv_a, recv_b, from_core, from_x, mine, other, bwd, turn, pole, out, rows_ref, sems,
):
    rows, tracers, levels, cols = base.shape
    half_lev = levels // 2
    n_half = tracers * half_lev
    half = bwd.shape[1] // 2
    south, polar, even = latitude_role(lat_count)
    lon, own, right_core = longitude_role()

    @pl.when(polar)
    def _():
        copies = []

        def leave(k, row):
            copies.append(pltpu.make_async_copy(rows_ref.at[k], out.at[row], sems.at[k]))
            copies[-1].start()

        first, second = mine[...], other[...]
        near = own == 0
        halves = jnp.where(near, first, second), jnp.where(near, second, first)
        cos, sin = pole[lon, 1:2], pole[lon, 2:3]
        at = KF % LANE
        for t in range(tracers):
            for h in (0, 1):
                p = halves[h][t * half_lev : (t + 1) * half_lev, half - LANE : half]
                c0, c1, s1 = p[:, at : at + 1], p[:, at + 1 : at + 2], p[:, at + 2 : at + 3]
                y = (1.0 / circle) * c0 + (2.0 / circle) * (c1 * cos + s1 * sin)
                rows_ref[3, t, h * half_lev : (h + 1) * half_lev, :] = y[:, :cols]
        leave(3, jnp.where(south, rows - 1, 0))
        places = [jnp.where(south, rows - 2 - slot, slot + 1) for slot in range(3)]
        blocks = []
        for slot, row in enumerate(places):
            kept = jnp.where(south, cutoff[1, row], cutoff[0, row])
            for h in (0, 1):
                block = halves[h][slot * n_half : (slot + 1) * n_half]
                blocks.append(weighted(block, kept, circle, turn, lon))
        y = dot3(jnp.concatenate(blocks), bwd)
        for slot, row in enumerate(places):
            place(rows_ref, slot, y[2 * slot * n_half : 2 * (slot + 1) * n_half], cols, half_lev)
            leave(slot, row)
        for copy in copies:
            copy.wait()

    @pl.when(jnp.logical_not(polar))
    def _():
        row = lax.broadcasted_iota(jnp.int32, (8, LANE), 0)
        lane = lax.broadcasted_iota(jnp.int32, (8, LANE), 1)
        start = cols // LANE * LANE
        low = jnp.where((row == 1) & (lane == 0), 1.0, 0.0).astype(jnp.float32)
        high = jnp.where((row == 0) & (lane == cols - 1 - start), 1.0, 0.0).astype(jnp.float32)
        dims = (((0,), (0,)), ((), ()))
        exact = lax.Precision.HIGHEST
        count = rows * tracers * levels
        core_side, x_side = from_core[:8, :count], from_x[:8, :count]
        left = jnp.where(right_core, x_side, core_side)
        right = jnp.where(right_core, core_side, x_side)
        first = lax.dot_general(left, low, dims, precision=exact, preferred_element_type=jnp.float32)
        end = lax.dot_general(right, high, dims, precision=exact, preferred_element_type=jnp.float32)
        shape = (rows, tracers, levels, LANE)
        first, end = first.reshape(shape), end.reshape(shape)
        side_a = recv_a[...]
        side_b = recv_b[:, :cols].reshape(tracers, levels, cols)
        copies = []
        for r in range(rows):
            value = base[r]
            if r == rows - 1:
                value = value + jnp.where(even, side_a, side_b)
            if r == 0:
                value = value - jnp.where(even, side_b, side_a)
            rows_ref[r] = value
            rows_ref[r, :, :, :LANE] -= first[r]
            rows_ref[r, :, :, start:] += end[r][..., : cols - start]
            copies.append(pltpu.make_async_copy(rows_ref.at[r], out.at[r], sems.at[r]))
            copies[-1].start()
        for copy in copies:
            copy.wait()


def fast_body(adj, east, north, cutoff):
    lat_count, lon_count = lax.axis_size("lat"), lax.axis_size("lon")
    rows, tracers, levels, cols = adj.shape
    circle = cols * lon_count
    fwd, bwd, turn, pole = tables(cols, circle, lon_count)
    wide, width = fwd.shape[1:]
    last = lat_count - 1
    f32 = jnp.float32
    params = pltpu.CompilerParams(vmem_limit_bytes=40 << 20)
    dma = pltpu.SemaphoreType.DMA
    vmem = pl.BlockSpec(memory_space=VMEM)
    smem = pl.BlockSpec(memory_space=pltpu.SMEM)
    anywhere = pl.BlockSpec(memory_space=pl.ANY)
    far = pl.BlockSpec(memory_space=HBM)
    n_half = tracers * levels // 2
    pair, single = (2 * n_half, width), (n_half, width)

    def put(x, space):
        return pltpu.with_memory_space_constraint(x, space)

    def call(kernel, outs, *args, scratch=(), cost=LIGHT):
        return pl.pallas_call(
            functools.partial(kernel, lat_count),
            out_shape=[VMEM(s, f32) for s in outs],
            in_specs=[vmem] * len(args),
            out_specs=[vmem] * len(outs),
            scratch_shapes=[VMEM(s, f32) for s in scratch],
            compiler_params=params,
            cost_estimate=cost,
        )(*(put(x, VMEM) for x in args))

    lats, lons = range(lat_count), range(lon_count)

    def swap(x, pairs):
        return lax.ppermute(x, ("lat", "lon"), [(a * lon_count + i, b * lon_count + j) for a, i, b, j in pairs])

    by_core = [(a, i, a, i ^ 1) for a in lats for i in lons]
    by_x = [(a, i, a, i ^ 2) for a in lats for i in lons]
    by_lat = [(a, i, a ^ 1, i) for a in lats for i in lons]
    mixed = [(a, i, a, i ^ 2) if a in (0, last) else (a, i, ((a + 1) ^ 1) - 1, i) for a in lats for i in lons]

    edge = pl.pallas_call(
        functools.partial(edge_kernel, lat_count),
        out_shape=VMEM(adj.shape[1:], f32),
        in_specs=[far] * 2,
        out_specs=vmem,
        scratch_shapes=[VMEM(adj.shape[1:], f32), VMEM(north.shape[1:], f32), dma((2,))],
        compiler_params=params,
    )(put(adj, HBM), put(north, HBM))
    recv_a = swap(edge, by_lat)
    base, keep, send, local, fwd, turn = pl.pallas_call(
        functools.partial(local_kernel, lat_count),
        out_shape=[VMEM(s, f32) for s in (adj.shape, pair, pair, (2 * n_half, wide))]
        + [VMEM(fwd.shape, jnp.bfloat16), VMEM(turn.shape, f32)],
        in_specs=[anywhere] + [far] * 6,
        out_specs=[vmem] * 6,
        scratch_shapes=[
            VMEM(shape, f32)
            for shape in (
                adj.shape,
                east.shape,
                north.shape,
                pole.shape,
                (levels, wide),
                (rows, 2, tracers, levels // 2, wide),
                (rows, tracers, levels, LANE),
            )
        ]
        + [dma((6,))],
        compiler_params=params,
        cost_estimate=LIGHT,
    )(put(edge, VMEM), *(put(x, HBM) for x in (adj, east, north, fwd, turn, pole)))
    got = swap(send, by_core)
    def token(*args):
        return pl.pallas_call(
            token_kernel,
            out_shape=VMEM((8, LANE), f32),
            in_specs=[vmem] * len(args),
            out_specs=vmem,
            compiler_params=params,
            cost_estimate=HEAVY,
        )(*(put(x, VMEM) for x in args))

    (part,) = call(sum_kernel, (pair,), keep, got, token(local))
    across = swap(part, mixed)
    keep3, send3 = call(third_kernel, (single, single), local, recv_a, got, part, fwd, turn, scratch=((2 * n_half, wide),))
    got3 = swap(send3, by_core)
    (part3,) = call(sum_kernel, (single,), keep3, got3, send3)
    across3 = swap(part3, by_x)
    (mine,) = call(total_kernel, ((3 * n_half, width),), part, across, part3, across3, token(part3, across))
    other = swap(mine, by_core)
    return pl.pallas_call(
        functools.partial(finish_kernel, lat_count, circle),
        out_shape=jax.ShapeDtypeStruct(adj.shape, f32),
        in_specs=[smem] + [vmem] * 10,
        out_specs=anywhere,
        scratch_shapes=[VMEM(adj.shape, f32), dma((rows,))],
        compiler_params=params,
    )(cutoff, *(put(x, VMEM) for x in (base, recv_a, across, got, across3, mine, other, bwd, turn, pole)))


full_precision = lax.Precision.HIGHEST


def extended(block, sides, width, periodic):
    for axis, dim in sides:
        count = lax.axis_size(axis)
        forward = [(i, i + 1) for i in range(count - 1)]
        if periodic:
            forward.append((count - 1, 0))
        backward = [(target, source) for source, target in forward]
        low = lax.ppermute(
            lax.slice_in_dim(block, block.shape[dim] - width, None, axis=dim), axis, forward
        )
        high = lax.ppermute(lax.slice_in_dim(block, 0, width, axis=dim), axis, backward)
        block = jnp.concatenate([low, block, high], axis=dim)
    return block


def from_partner(block, axis, stride):
    count = lax.axis_size(axis)
    route = []
    for low in range(count):
        high = low | 1 << stride
        if high != low and high < count:
            route += [(low, high), (high, low)]
    return lax.ppermute(block, axis, route)


def mode_table(columns, modes_kept, circle):
    wavenumber = jnp.arange(modes_kept, dtype=jnp.int32)
    product = columns[:, None] * wavenumber[None, :] % circle
    phases = product.astype(jnp.float32) * (2.0 * math.pi / circle)
    return jnp.concatenate([jnp.cos(phases), jnp.sin(phases)], axis=1)


def spectral_weights(latitude, cutoff, modes_kept, circle, total_lat):
    cap_lat = cutoff.shape[1]
    offsets = jnp.arange(cap_lat, dtype=jnp.int32)
    north_hit = latitude[..., None] == offsets
    south_hit = latitude[..., None] == total_lat - cap_lat + offsets
    chosen = jnp.sum(
        jnp.where(north_hit, cutoff[0], 0) + jnp.where(south_hit, cutoff[1], 0), axis=-1
    )
    wavenumber = jnp.arange(2 * modes_kept, dtype=jnp.int32) % modes_kept
    mode_weight = jnp.where(wavenumber == 0, 1.0, 2.0) / circle
    kept_mask = wavenumber <= chosen[..., None]
    return jnp.where(kept_mask, mode_weight, 0.0).astype(jnp.float32)


def general_body(adj_next, east_courant, north_courant, cutoff):
    lat_count = lax.axis_size("lat")
    lon_count = lax.axis_size("lon")
    lat_index = lax.axis_index("lat")
    lon_index = lax.axis_index("lon")
    lat_rows, tracers, levels, lon_cols = adj_next.shape
    circle = lon_cols * lon_count
    total_lat = lat_rows * lat_count
    modes_kept = KF
    cap_lat = cutoff.shape[1]
    zonal_flux = east_courant[:, None] * adj_next
    meridional = north_courant[:, None] * adj_next
    lon_padded = extended(zonal_flux, (("lon", 3),), 1, True)
    result = adj_next + lon_padded[..., 2:] - lon_padded[..., :-2]
    lat_padded = extended(meridional, (("lat", 0),), 1, False)
    result = result + lat_padded[2:] - lat_padded[:-2]
    edge_row = jnp.where(lat_index == 0, meridional[0], meridional[-1])
    pole_bit = lon_count.bit_length() - 2
    partner = from_partner(edge_row, "lon", pole_bit)
    north_sign = jnp.where(lat_index == 0, 1.0, 0.0).astype(jnp.float32)
    south_sign = jnp.where(lat_index == lat_count - 1, -1.0, 0.0).astype(jnp.float32)
    result = result.at[0].add(north_sign * partner)
    result = result.at[-1].add(south_sign * partner)
    latitude = lat_index * lat_rows + jnp.arange(lat_rows, dtype=jnp.int32)
    in_cap = (latitude < cap_lat) | (latitude >= total_lat - cap_lat)
    local_cols = lon_index * lon_cols + jnp.arange(lon_cols, dtype=jnp.int32)
    local_table = mode_table(local_cols, modes_kept, circle)
    weights = spectral_weights(latitude, cutoff, modes_kept, circle, total_lat)
    partial_sum = jnp.einsum(
        "acvn,nk->acvk",
        result,
        local_table,
        precision=full_precision,
        preferred_element_type=jnp.float32,
    )
    level_share = lax.psum_scatter(partial_sum, "lon", scatter_dimension=2, tiled=True)
    level_share = level_share * weights[:, None, None, :]
    totals = lax.all_gather(level_share, "lon", axis=2, tiled=True)
    rebuilt = jnp.einsum(
        "acvk,nk->acvn",
        totals,
        local_table,
        precision=full_precision,
        preferred_element_type=jnp.float32,
    )
    output = jnp.where(in_cap[:, None, None, None], rebuilt, result)
    return output


def body(adj, east, north, cutoff):
    lat_count, lon_count = lax.axis_size("lat"), lax.axis_size("lon")
    one_band = cutoff.shape[1] == adj.shape[0] == 4
    if one_band and lon_count == 4 and lat_count % 2 == 0 and lat_count >= 4 and adj.shape[2] % 16 == 0:
        return fast_body(adj, east, north, cutoff)
    return general_body(adj, east, north, cutoff)


def solution(mesh):
    return jax.shard_map(
        body,
        mesh=mesh,
        in_specs=(P("lat", None, None, "lon"), P("lat", None, "lon"), P("lat", None, "lon"), P()),
        out_specs=P("lat", None, None, "lon"),
        check_vma=False,
    )
```

```python
import functools
import math

import jax
import jax.numpy as jnp
import ml_dtypes
import numpy as np
from jax import lax
from jax.experimental import pallas as pl
from jax.experimental.pallas import tpu as pltpu
from jax.sharding import PartitionSpec as P

KF = 352
LANE = 128
VMEM = pltpu.VMEM
HBM = pltpu.HBM
HEAVY = pl.CostEstimate(flops=2**37, bytes_accessed=0, transcendentals=0)
LIGHT = pl.CostEstimate(flops=0, bytes_accessed=1000, transcendentals=0)


def ceil_to(value, unit):
    return -(-value // unit) * unit


def split16(table):
    high = table.astype(ml_dtypes.bfloat16)
    low = (table - high.astype(np.float64)).astype(ml_dtypes.bfloat16)
    return np.stack([high, low])


def tables(cols, circle, lon_count):
    wide = ceil_to(cols + 2, LANE)
    half = ceil_to(KF + 2, LANE)
    place = np.zeros(wide, np.int64)
    place[: cols + 1] = np.arange(cols + 1)
    place[-1] = -1
    live = np.zeros(wide)
    live[: cols + 1] = 1
    live[-1] = 1
    mode = np.arange(KF)
    phase = 2 * np.pi * ((place[:, None] * mode[None]) % circle) / circle
    forward = np.zeros((wide, 2 * half))
    forward[:, :KF] = np.cos(phase) * live[:, None]
    forward[:, half : half + KF] = np.sin(phase) * live[:, None]
    backward = forward.T.copy()
    backward[:, cols:] = 0
    turn = np.zeros((lon_count, 2, half), np.float32)
    angle = 2 * np.pi * ((np.arange(lon_count)[:, None] * mode[None]) % lon_count) / lon_count
    turn[:, 0, :KF] = np.cos(angle)
    turn[:, 1, :KF] = np.sin(angle)
    pole = np.zeros((lon_count, 4, wide), np.float32)
    for index in range(lon_count):
        first = 2 * np.pi * (place + index * cols) / circle
        pole[index, 0] = live
        pole[index, 1] = np.cos(first) * live
        pole[index, 2] = np.sin(first) * live
    return split16(forward), split16(backward), turn, pole


def dot3(block, table_ref):
    rows = block.shape[0]
    high = block.astype(jnp.bfloat16)
    low = (block - high.astype(jnp.float32)).astype(jnp.bfloat16)
    stack = jnp.dot(jnp.concatenate([high, low]), table_ref[0], preferred_element_type=jnp.float32)
    return stack[:rows] + stack[rows:] + jnp.dot(high, table_ref[1], preferred_element_type=jnp.float32)


def latitude_role(lat_count):
    lat = lax.axis_index("lat")
    south = lat == lat_count - 1
    return south, jnp.logical_or(lat == 0, south), lax.rem(lat, 2) == 0


def longitude_role():
    lon = lax.axis_index("lon")
    core = lax.rem(lon, 2)
    return lon, core, core == 0


def turned(p, turn, lon):
    half = p.shape[1] // 2
    a, b = turn[lon, 0:1], turn[lon, 1:2]
    c, s = p[:, :half], p[:, half:]
    return c * a - s * b, s * a + c * b


def weighted(block, kept, circle, turn, lon):
    half = block.shape[1] // 2
    wave = lax.broadcasted_iota(jnp.int32, (1, half), 1)
    weight = jnp.where(wave <= kept, jnp.where(wave == 0, 1.0 / circle, 2.0 / circle), 0.0).astype(jnp.float32)
    wa, wb = weight * turn[lon, 0:1], weight * turn[lon, 1:2]
    c, s = block[:, :half], block[:, half:]
    return jnp.concatenate([c * wa + s * wb, s * wa - c * wb], axis=1)


def edge_kernel(lat_count, adj_hbm, north_hbm, edge, adj, north, sems):
    _, _, even = latitude_role(lat_count)
    row = jnp.where(even, adj_hbm.shape[0] - 1, 0)
    copies = (
        pltpu.make_async_copy(adj_hbm.at[row], adj, sems.at[0]),
        pltpu.make_async_copy(north_hbm.at[row], north, sems.at[1]),
    )
    for copy in copies:
        copy.start()
    for copy in copies:
        copy.wait()
    edge[...] = north[...][None] * adj[...]


def local_kernel(
    lat_count, after, adj, east, north, fwd, turn, pole, base, edge, keep, send, third, flux, wide_x, ends
):
    rows, tracers, levels, cols = adj.shape
    wide = flux.shape[-1]
    south, polar, even = latitude_role(lat_count)
    lon, own, _ = longitude_role()
    half_lev = levels // 2
    n_half = tracers * half_lev
    half = fwd.shape[-1] // 2
    row_b = jnp.where(even, 0, rows - 1)
    flux[:, cols:] = jnp.zeros((levels, wide - cols), jnp.float32)

    def transported(r, t):
        out = adj[r, t]
        if r + 1 < rows:
            out = out + north[r + 1] * adj[r + 1, t]
        if r > 0:
            out = out - north[r - 1] * adj[r - 1, t]
        return out

    def spread(r, t):
        flux[:, :cols] = east[r] * adj[r, t]
        f = flux[...]
        return pltpu.roll(f, wide - 1, 1) - pltpu.roll(f, 1, 1), f

    @pl.when(jnp.logical_not(polar))
    def _():
        start = cols // LANE * LANE
        lane = lax.broadcasted_iota(jnp.int32, (levels, LANE), 1)
        at = cols - 1 - start
        for r in range(rows):
            for t in range(tracers):
                move, f = spread(r, t)
                base[r, t] = transported(r, t) + move[:, :cols]
                ends[r, t] = jnp.where(lane == 0, f[:, :LANE], jnp.where(lane == at, f[:, start : start + LANE], 0.0))
        row = lax.broadcasted_iota(jnp.int32, (8, LANE), 0)
        lane = lax.broadcasted_iota(jnp.int32, (8, LANE), 1)
        pick = jnp.where((row == 0) & (lane == 0) | (row == 1) & (lane == at), 1.0, 0.0).astype(jnp.float32)
        sides = lax.dot_general(
            pick,
            ends[...].reshape(rows * tracers * levels, LANE),
            (((1,), (1,)), ((), ())),
            precision=lax.Precision.HIGHEST,
            preferred_element_type=jnp.float32,
        )
        send[:8, : sides.shape[1]] = sides
        edge[...] = north[row_b][None] * adj[row_b]

    @pl.when(polar)
    def _():
        for r in range(rows):
            near = jnp.where(south, rows - 1 - r, r)
            slot = lax.rem(near + rows - 1, rows)
            for t in range(tracers):
                move, _ = spread(r, t)
                for h in (0, 1):
                    part = slice(h * half_lev, (h + 1) * half_lev)
                    where = jnp.where(own == h, 0, 1)
                    wide_x[slot, where, t] = move[part]
                    wide_x[slot, where, t, :, :cols] += transported(r, t)[part]
        c, s = turned(dot3(wide_x[:2].reshape(4 * n_half, wide), fwd), turn, lon)
        for slot in range(2):
            spot = slice(slot * n_half, (slot + 1) * n_half)
            first = slice(2 * slot * n_half, (2 * slot + 1) * n_half)
            second = slice((2 * slot + 1) * n_half, (2 * slot + 2) * n_half)
            keep[spot, :half], keep[spot, half:] = c[first], s[first]
            send[spot, :half], send[spot, half:] = c[second], s[second]
        third[...] = wide_x[2].reshape(tracers * levels, wide)
        sign = jnp.where(south, -1.0, 1.0).astype(jnp.float32)
        row_p = jnp.where(south, rows - 1, 0)
        lane = lax.broadcasted_iota(jnp.int32, (half_lev, LANE), 1)
        one, cos, sin = (pole[lon, k : k + 1] for k in range(3))
        for t in range(tracers):
            m = north[row_p] * adj[row_p, t] * sign
            for k, target in ((0, keep), (1, send)):
                u = wide_x[3, k, t]
                flux[:half_lev, :cols] = jnp.where(own == k, m[:half_lev], m[half_lev:])
                v = flux[:half_lev]
                c0 = jnp.sum((u + v) * one, axis=1, keepdims=True)
                c1 = jnp.sum((u - v) * cos, axis=1, keepdims=True)
                s1 = jnp.sum((u - v) * sin, axis=1, keepdims=True)
                at = KF % LANE
                lanes = slice(half - LANE, half)
                spot = slice(t * half_lev, (t + 1) * half_lev)
                target[spot, lanes] = jnp.where(
                    lane == at, c0, jnp.where(lane == at + 1, c1, jnp.where(lane == at + 2, s1, target[spot, lanes]))
                )


def third_kernel(lat_count, local, recv, after, fwd, turn, keep, send, block):
    tracers, levels, cols = recv.shape
    south, polar, _ = latitude_role(lat_count)
    lon, own, _ = longitude_role()
    half_lev = levels // 2
    n_half = tracers * half_lev
    half = fwd.shape[-1] // 2

    @pl.when(polar)
    def _():
        sign = jnp.where(south, -1.0, 1.0).astype(jnp.float32)
        block[...] = local[...]
        for t in range(tracers):
            m = recv[t] * sign
            for k in (0, 1):
                first = k * n_half + t * half_lev
                block[first : first + half_lev, :cols] += jnp.where(own == k, m[:half_lev], m[half_lev:])
        c, s = turned(dot3(block[...], fwd), turn, lon)
        keep[:, :half], keep[:, half:] = c[:n_half], s[:n_half]
        send[:, :half], send[:, half:] = c[n_half:], s[n_half:]


def token_kernel(x, *rest):
    rest[-1][...] = x[:8, :LANE]


def sum_kernel(lat_count, mine, got, after, out):
    _, polar, _ = latitude_role(lat_count)

    @pl.when(polar)
    def _():
        out[...] = mine[...] + got[...]

    @pl.when(jnp.logical_not(polar))
    def _():
        out[:8] = got[:8]


def total_kernel(lat_count, mine, across, after, out):
    _, polar, _ = latitude_role(lat_count)

    @pl.when(polar)
    def _():
        out[...] = mine[...] + across[...]


def place(rows_ref, k, y, cols, half_lev):
    y = y.reshape(2, -1, half_lev, y.shape[-1])
    for h in (0, 1):
        rows_ref[k, :, h * half_lev : (h + 1) * half_lev, :] = y[h][..., :cols]


def halves_of(mine, other, own):
    first, second = mine[...], other[...]
    near = own == 0
    return jnp.where(near, first, second), jnp.where(near, second, first)


def cap_kernel(lat_count, circle, cutoff, mine, other, bwd, turn, pole, out):
    _, tracers, levels, cols = out.shape
    half_lev = levels // 2
    n_half = tracers * half_lev
    half = bwd.shape[1] // 2
    rows = cutoff.shape[1]
    south, polar, _ = latitude_role(lat_count)
    lon, own, _ = longitude_role()

    @pl.when(polar)
    def _():
        halves = halves_of(mine, other, own)
        cos, sin = pole[lon, 1:2], pole[lon, 2:3]
        at = KF % LANE
        for t in range(tracers):
            for h in (0, 1):
                p = halves[h][t * half_lev : (t + 1) * half_lev, half - LANE : half]
                c0, c1, s1 = p[:, at : at + 1], p[:, at + 1 : at + 2], p[:, at + 2 : at + 3]
                y = (1.0 / circle) * c0 + (2.0 / circle) * (c1 * cos + s1 * sin)
                out[0, t, h * half_lev : (h + 1) * half_lev, :] = y[:, :cols]
        blocks = []
        for slot in range(2):
            row = jnp.where(south, rows - 2 - slot, slot + 1)
            kept = jnp.where(south, cutoff[1, row], cutoff[0, row])
            for h in (0, 1):
                block = halves[h][slot * n_half : (slot + 1) * n_half]
                blocks.append(weighted(block, kept, circle, turn, lon))
        y = dot3(jnp.concatenate(blocks), bwd)
        for slot in range(2):
            place(out, slot + 1, y[2 * slot * n_half : 2 * (slot + 1) * n_half], cols, half_lev)


def finish_kernel(
    lat_count, circle, cutoff, caps, base, recv_a, recv_b, from_core, from_x, mine, other, bwd, turn, out, rows_ref, sems,
):
    rows, tracers, levels, cols = base.shape
    half_lev = levels // 2
    south, polar, even = latitude_role(lat_count)
    lon, own, right_core = longitude_role()

    @pl.when(polar)
    def _():
        copies = []
        for near in range(rows - 1):
            row = jnp.where(south, rows - 1 - near, near)
            copies.append(pltpu.make_async_copy(caps.at[near], out.at[row], sems.at[near]))
            copies[-1].start()
        row = jnp.where(south, 0, rows - 1)
        kept = jnp.where(south, cutoff[1, row], cutoff[0, row])
        blocks = [weighted(block, kept, circle, turn, lon) for block in halves_of(mine, other, own)]
        place(rows_ref, 0, dot3(jnp.concatenate(blocks), bwd), cols, half_lev)
        copies.append(pltpu.make_async_copy(rows_ref.at[0], out.at[row], sems.at[rows - 1]))
        copies[-1].start()
        for copy in copies:
            copy.wait()

    @pl.when(jnp.logical_not(polar))
    def _():
        row = lax.broadcasted_iota(jnp.int32, (8, LANE), 0)
        lane = lax.broadcasted_iota(jnp.int32, (8, LANE), 1)
        start = cols // LANE * LANE
        low = jnp.where((row == 1) & (lane == 0), 1.0, 0.0).astype(jnp.float32)
        high = jnp.where((row == 0) & (lane == cols - 1 - start), 1.0, 0.0).astype(jnp.float32)
        dims = (((0,), (0,)), ((), ()))
        exact = lax.Precision.HIGHEST
        count = rows * tracers * levels
        core_side, x_side = from_core[:8, :count], from_x[:8, :count]
        left = jnp.where(right_core, x_side, core_side)
        right = jnp.where(right_core, core_side, x_side)
        first = lax.dot_general(left, low, dims, precision=exact, preferred_element_type=jnp.float32)
        end = lax.dot_general(right, high, dims, precision=exact, preferred_element_type=jnp.float32)
        shape = (rows, tracers, levels, LANE)
        first, end = first.reshape(shape), end.reshape(shape)
        side_a = recv_a[...]
        side_b = recv_b[...]
        copies = []
        for r in range(rows):
            value = base[r]
            if r == rows - 1:
                value = value + jnp.where(even, side_a, side_b)
            if r == 0:
                value = value - jnp.where(even, side_b, side_a)
            rows_ref[r] = value
            rows_ref[r, :, :, :LANE] -= first[r]
            rows_ref[r, :, :, start:] += end[r][..., : cols - start]
            copies.append(pltpu.make_async_copy(rows_ref.at[r], out.at[r], sems.at[r]))
            copies[-1].start()
        for copy in copies:
            copy.wait()


def fast_body(adj, east, north, cutoff):
    lat_count, lon_count = lax.axis_size("lat"), lax.axis_size("lon")
    rows, tracers, levels, cols = adj.shape
    circle = cols * lon_count
    fwd, bwd, turn, pole = tables(cols, circle, lon_count)
    wide, width = fwd.shape[1:]
    last = lat_count - 1
    f32 = jnp.float32
    params = pltpu.CompilerParams(vmem_limit_bytes=40 << 20)
    dma = pltpu.SemaphoreType.DMA
    vmem = pl.BlockSpec(memory_space=VMEM)
    smem = pl.BlockSpec(memory_space=pltpu.SMEM)
    anywhere = pl.BlockSpec(memory_space=pl.ANY)
    far = pl.BlockSpec(memory_space=HBM)
    n_half = tracers * levels // 2
    pair, single = (2 * n_half, width), (n_half, width)

    def put(x, space):
        return pltpu.with_memory_space_constraint(x, space)

    def call(kernel, outs, *args, scratch=(), cost=LIGHT):
        return pl.pallas_call(
            functools.partial(kernel, lat_count),
            out_shape=[VMEM(s, f32) for s in outs],
            in_specs=[vmem] * len(args),
            out_specs=[vmem] * len(outs),
            scratch_shapes=[VMEM(s, f32) for s in scratch],
            compiler_params=params,
            cost_estimate=cost,
        )(*(put(x, VMEM) for x in args))

    lats, lons = range(lat_count), range(lon_count)

    def swap(x, pairs):
        return lax.ppermute(x, ("lat", "lon"), [(a * lon_count + i, b * lon_count + j) for a, i, b, j in pairs])

    by_core = [(a, i, a, i ^ 1) for a in lats for i in lons]
    by_x = [(a, i, a, i ^ 2) for a in lats for i in lons]
    by_lat = [(a, i, a ^ 1, i) for a in lats for i in lons]
    by_next = [(a, i, ((a + 1) ^ 1) - 1, i) for a in range(1, last) for i in lons]

    edge = pl.pallas_call(
        functools.partial(edge_kernel, lat_count),
        out_shape=VMEM(adj.shape[1:], f32),
        in_specs=[far] * 2,
        out_specs=vmem,
        scratch_shapes=[VMEM(adj.shape[1:], f32), VMEM(north.shape[1:], f32), dma((2,))],
        cost_estimate=HEAVY,
        compiler_params=params,
    )(put(adj, HBM), put(north, HBM))
    recv_a = swap(edge, by_lat)
    base, edge_b, keep, send, local = call(
        local_kernel,
        (adj.shape, adj.shape[1:], pair, pair, (2 * n_half, wide)),
        edge,
        adj,
        east,
        north,
        fwd,
        turn,
        pole,
        scratch=((levels, wide), (rows, 2, tracers, levels // 2, wide), (rows, tracers, levels, LANE)),
    )
    got = swap(send, by_core)
    def token(*args):
        return pl.pallas_call(
            token_kernel,
            out_shape=VMEM((8, LANE), f32),
            in_specs=[vmem] * len(args),
            out_specs=vmem,
            compiler_params=params,
            cost_estimate=HEAVY,
        )(*(put(x, VMEM) for x in args))

    (part,) = call(sum_kernel, (pair,), keep, got, token(local))
    across = swap(part, by_x)
    recv_b = swap(edge_b, by_next)
    keep3, send3 = call(third_kernel, (single, single), local, recv_a, part, fwd, turn, scratch=((2 * n_half, wide),))
    got3 = swap(send3, by_core)
    (part3,) = call(sum_kernel, (single,), keep3, got3, send3)
    across3 = swap(part3, by_x)
    (mine,) = call(total_kernel, (pair,), part, across, part3)
    other = swap(mine, by_core)
    (mine3,) = call(total_kernel, (single,), part3, across3, token(part3, across, recv_b))
    other3 = swap(mine3, by_core)
    caps = pl.pallas_call(
        functools.partial(cap_kernel, lat_count, circle),
        out_shape=VMEM((3,) + adj.shape[1:], f32),
        in_specs=[smem] + [vmem] * 5,
        out_specs=vmem,
        compiler_params=params,
    )(cutoff, *(put(x, VMEM) for x in (mine, other, bwd, turn, pole)))
    return pl.pallas_call(
        functools.partial(finish_kernel, lat_count, circle),
        out_shape=jax.ShapeDtypeStruct(adj.shape, f32),
        in_specs=[smem] + [vmem] * 10,
        out_specs=anywhere,
        scratch_shapes=[VMEM(adj.shape, f32), dma((rows,))],
        compiler_params=params,
    )(cutoff, *(put(x, VMEM) for x in (caps, base, recv_a, recv_b, got, across, mine3, other3, bwd, turn)))


full_precision = lax.Precision.HIGHEST


def extended(block, sides, width, periodic):
    for axis, dim in sides:
        count = lax.axis_size(axis)
        forward = [(i, i + 1) for i in range(count - 1)]
        if periodic:
            forward.append((count - 1, 0))
        backward = [(target, source) for source, target in forward]
        low = lax.ppermute(
            lax.slice_in_dim(block, block.shape[dim] - width, None, axis=dim), axis, forward
        )
        high = lax.ppermute(lax.slice_in_dim(block, 0, width, axis=dim), axis, backward)
        block = jnp.concatenate([low, block, high], axis=dim)
    return block


def from_partner(block, axis, stride):
    count = lax.axis_size(axis)
    route = []
    for low in range(count):
        high = low | 1 << stride
        if high != low and high < count:
            route += [(low, high), (high, low)]
    return lax.ppermute(block, axis, route)


def mode_table(columns, modes_kept, circle):
    wavenumber = jnp.arange(modes_kept, dtype=jnp.int32)
    product = columns[:, None] * wavenumber[None, :] % circle
    phases = product.astype(jnp.float32) * (2.0 * math.pi / circle)
    return jnp.concatenate([jnp.cos(phases), jnp.sin(phases)], axis=1)


def spectral_weights(latitude, cutoff, modes_kept, circle, total_lat):
    cap_lat = cutoff.shape[1]
    offsets = jnp.arange(cap_lat, dtype=jnp.int32)
    north_hit = latitude[..., None] == offsets
    south_hit = latitude[..., None] == total_lat - cap_lat + offsets
    chosen = jnp.sum(
        jnp.where(north_hit, cutoff[0], 0) + jnp.where(south_hit, cutoff[1], 0), axis=-1
    )
    wavenumber = jnp.arange(2 * modes_kept, dtype=jnp.int32) % modes_kept
    mode_weight = jnp.where(wavenumber == 0, 1.0, 2.0) / circle
    kept_mask = wavenumber <= chosen[..., None]
    return jnp.where(kept_mask, mode_weight, 0.0).astype(jnp.float32)


def general_body(adj_next, east_courant, north_courant, cutoff):
    lat_count = lax.axis_size("lat")
    lon_count = lax.axis_size("lon")
    lat_index = lax.axis_index("lat")
    lon_index = lax.axis_index("lon")
    lat_rows, tracers, levels, lon_cols = adj_next.shape
    circle = lon_cols * lon_count
    total_lat = lat_rows * lat_count
    modes_kept = KF
    cap_lat = cutoff.shape[1]
    zonal_flux = east_courant[:, None] * adj_next
    meridional = north_courant[:, None] * adj_next
    lon_padded = extended(zonal_flux, (("lon", 3),), 1, True)
    result = adj_next + lon_padded[..., 2:] - lon_padded[..., :-2]
    lat_padded = extended(meridional, (("lat", 0),), 1, False)
    result = result + lat_padded[2:] - lat_padded[:-2]
    edge_row = jnp.where(lat_index == 0, meridional[0], meridional[-1])
    pole_bit = lon_count.bit_length() - 2
    partner = from_partner(edge_row, "lon", pole_bit)
    north_sign = jnp.where(lat_index == 0, 1.0, 0.0).astype(jnp.float32)
    south_sign = jnp.where(lat_index == lat_count - 1, -1.0, 0.0).astype(jnp.float32)
    result = result.at[0].add(north_sign * partner)
    result = result.at[-1].add(south_sign * partner)
    latitude = lat_index * lat_rows + jnp.arange(lat_rows, dtype=jnp.int32)
    in_cap = (latitude < cap_lat) | (latitude >= total_lat - cap_lat)
    local_cols = lon_index * lon_cols + jnp.arange(lon_cols, dtype=jnp.int32)
    local_table = mode_table(local_cols, modes_kept, circle)
    weights = spectral_weights(latitude, cutoff, modes_kept, circle, total_lat)
    partial_sum = jnp.einsum(
        "acvn,nk->acvk",
        result,
        local_table,
        precision=full_precision,
        preferred_element_type=jnp.float32,
    )
    level_share = lax.psum_scatter(partial_sum, "lon", scatter_dimension=2, tiled=True)
    level_share = level_share * weights[:, None, None, :]
    totals = lax.all_gather(level_share, "lon", axis=2, tiled=True)
    rebuilt = jnp.einsum(
        "acvk,nk->acvn",
        totals,
        local_table,
        precision=full_precision,
        preferred_element_type=jnp.float32,
    )
    output = jnp.where(in_cap[:, None, None, None], rebuilt, result)
    return output


def body(adj, east, north, cutoff):
    lat_count, lon_count = lax.axis_size("lat"), lax.axis_size("lon")
    one_band = cutoff.shape[1] == adj.shape[0] == 4
    if one_band and lon_count == 4 and lat_count % 2 == 0 and lat_count >= 4 and adj.shape[2] % 16 == 0:
        return fast_body(adj, east, north, cutoff)
    return general_body(adj, east, north, cutoff)


def solution(mesh):
    return jax.shard_map(
        body,
        mesh=mesh,
        in_specs=(P("lat", None, None, "lon"), P("lat", None, "lon"), P("lat", None, "lon"), P()),
        out_specs=P("lat", None, None, "lon"),
        check_vma=False,
    )
```

```python
import functools
import math

import jax
import jax.numpy as jnp
import ml_dtypes
import numpy as np
from jax import lax
from jax.experimental import pallas as pl
from jax.experimental.pallas import tpu as pltpu
from jax.sharding import PartitionSpec as P

KF = 352
LANE = 128
VMEM = pltpu.VMEM
HBM = pltpu.HBM
HEAVY = pl.CostEstimate(flops=2**37, bytes_accessed=0, transcendentals=0)
LIGHT = pl.CostEstimate(flops=0, bytes_accessed=1000, transcendentals=0)


def ceil_to(value, unit):
    return -(-value // unit) * unit


def split16(table):
    high = table.astype(ml_dtypes.bfloat16)
    low = (table - high.astype(np.float64)).astype(ml_dtypes.bfloat16)
    return np.stack([high, low])


def tables(cols, circle, lon_count):
    wide = ceil_to(cols + 2, LANE)
    half = ceil_to(KF + 2, LANE)
    place = np.zeros(wide, np.int64)
    place[: cols + 1] = np.arange(cols + 1)
    place[-1] = -1
    live = np.zeros(wide)
    live[: cols + 1] = 1
    live[-1] = 1
    mode = np.arange(KF)
    phase = 2 * np.pi * ((place[:, None] * mode[None]) % circle) / circle
    forward = np.zeros((wide, 2 * half))
    forward[:, :KF] = np.cos(phase) * live[:, None]
    forward[:, half : half + KF] = np.sin(phase) * live[:, None]
    backward = forward.T.copy()
    backward[:, cols:] = 0
    turn = np.zeros((lon_count, 2, half), np.float32)
    angle = 2 * np.pi * ((np.arange(lon_count)[:, None] * mode[None]) % lon_count) / lon_count
    turn[:, 0, :KF] = np.cos(angle)
    turn[:, 1, :KF] = np.sin(angle)
    pole = np.zeros((lon_count, 4, wide), np.float32)
    for index in range(lon_count):
        first = 2 * np.pi * (place + index * cols) / circle
        pole[index, 0] = live
        pole[index, 1] = np.cos(first) * live
        pole[index, 2] = np.sin(first) * live
    return split16(forward), split16(backward), turn, pole


def dot3(block, table_ref):
    rows = block.shape[0]
    high = block.astype(jnp.bfloat16)
    low = (block - high.astype(jnp.float32)).astype(jnp.bfloat16)
    stack = jnp.dot(jnp.concatenate([high, low]), table_ref[0], preferred_element_type=jnp.float32)
    return stack[:rows] + stack[rows:] + jnp.dot(high, table_ref[1], preferred_element_type=jnp.float32)


def latitude_role(lat_count):
    lat = lax.axis_index("lat")
    south = lat == lat_count - 1
    return south, jnp.logical_or(lat == 0, south), lax.rem(lat, 2) == 0


def longitude_role():
    lon = lax.axis_index("lon")
    core = lax.rem(lon, 2)
    return lon, core, core == 0


def turned(p, turn, lon):
    half = p.shape[1] // 2
    a, b = turn[lon, 0:1], turn[lon, 1:2]
    c, s = p[:, :half], p[:, half:]
    return c * a - s * b, s * a + c * b


def weighted(block, weights):
    half = block.shape[1] // 2
    c, s = block[:, :half], block[:, half:]
    return jnp.concatenate([c * weights[0:1] + s * weights[1:2], s * weights[0:1] - c * weights[1:2]], axis=1)


def weight_kernel(lat_count, circle, cutoff, after, turn, out):
    rows = cutoff.shape[1]
    south, polar, _ = latitude_role(lat_count)
    lon = lax.axis_index("lon")
    wave = lax.broadcasted_iota(jnp.int32, (1, turn.shape[-1]), 1)

    @pl.when(polar)
    def _():
        for slot in range(rows - 1):
            row = jnp.where(south, rows - 2 - slot, slot + 1)
            kept = jnp.where(south, cutoff[1, row], cutoff[0, row])
            weight = jnp.where(wave <= kept, jnp.where(wave == 0, 1.0 / circle, 2.0 / circle), 0.0).astype(jnp.float32)
            for k in (0, 1):
                out[slot, k : k + 1] = weight * turn[lon, k : k + 1]


def edge_kernel(lat_count, adj_hbm, north_hbm, edge, adj, north, sems):
    _, _, even = latitude_role(lat_count)
    row = jnp.where(even, adj_hbm.shape[0] - 1, 0)
    copies = (
        pltpu.make_async_copy(adj_hbm.at[row], adj, sems.at[0]),
        pltpu.make_async_copy(north_hbm.at[row], north, sems.at[1]),
    )
    for copy in copies:
        copy.start()
    for copy in copies:
        copy.wait()
    edge[...] = north[...][None] * adj[...]


def local_kernel(
    lat_count, after, adj, east, north, fwd, turn, pole, base, edge, keep, send, third, flux, wide_x, ends
):
    rows, tracers, levels, cols = adj.shape
    wide = flux.shape[-1]
    south, polar, even = latitude_role(lat_count)
    lon, own, _ = longitude_role()
    half_lev = levels // 2
    n_half = tracers * half_lev
    half = fwd.shape[-1] // 2
    row_b = jnp.where(even, 0, rows - 1)
    flux[:, cols:] = jnp.zeros((levels, wide - cols), jnp.float32)

    def transported(r, t):
        out = adj[r, t]
        if r + 1 < rows:
            out = out + north[r + 1] * adj[r + 1, t]
        if r > 0:
            out = out - north[r - 1] * adj[r - 1, t]
        return out

    def spread(r, t):
        flux[:, :cols] = east[r] * adj[r, t]
        f = flux[...]
        return pltpu.roll(f, wide - 1, 1) - pltpu.roll(f, 1, 1), f

    @pl.when(jnp.logical_not(polar))
    def _():
        start = cols // LANE * LANE
        lane = lax.broadcasted_iota(jnp.int32, (levels, LANE), 1)
        at = cols - 1 - start
        for r in range(rows):
            for t in range(tracers):
                move, f = spread(r, t)
                base[r, t] = transported(r, t) + move[:, :cols]
                ends[r, t] = jnp.where(lane == 0, f[:, :LANE], jnp.where(lane == at, f[:, start : start + LANE], 0.0))
        row = lax.broadcasted_iota(jnp.int32, (8, LANE), 0)
        lane = lax.broadcasted_iota(jnp.int32, (8, LANE), 1)
        pick = jnp.where((row == 0) & (lane == 0) | (row == 1) & (lane == at), 1.0, 0.0).astype(jnp.float32)
        sides = lax.dot_general(
            pick,
            ends[...].reshape(rows * tracers * levels, LANE),
            (((1,), (1,)), ((), ())),
            precision=lax.Precision.HIGHEST,
            preferred_element_type=jnp.float32,
        )
        send[:8, : sides.shape[1]] = sides
        edge[...] = north[row_b][None] * adj[row_b]

    @pl.when(polar)
    def _():
        for r in range(rows):
            near = jnp.where(south, rows - 1 - r, r)
            slot = lax.rem(near + rows - 1, rows)
            for t in range(tracers):
                move, _ = spread(r, t)
                for h in (0, 1):
                    part = slice(h * half_lev, (h + 1) * half_lev)
                    where = jnp.where(own == h, 0, 1)
                    wide_x[slot, where, t] = move[part]
                    wide_x[slot, where, t, :, :cols] += transported(r, t)[part]
        c, s = turned(dot3(wide_x[:2].reshape(4 * n_half, wide), fwd), turn, lon)
        for slot in range(2):
            spot = slice(slot * n_half, (slot + 1) * n_half)
            first = slice(2 * slot * n_half, (2 * slot + 1) * n_half)
            second = slice((2 * slot + 1) * n_half, (2 * slot + 2) * n_half)
            keep[spot, :half], keep[spot, half:] = c[first], s[first]
            send[spot, :half], send[spot, half:] = c[second], s[second]
        third[...] = wide_x[2].reshape(tracers * levels, wide)
        sign = jnp.where(south, -1.0, 1.0).astype(jnp.float32)
        row_p = jnp.where(south, rows - 1, 0)
        lane = lax.broadcasted_iota(jnp.int32, (half_lev, LANE), 1)
        one, cos, sin = (pole[lon, k : k + 1] for k in range(3))
        for t in range(tracers):
            m = north[row_p] * adj[row_p, t] * sign
            for k, target in ((0, keep), (1, send)):
                u = wide_x[3, k, t]
                flux[:half_lev, :cols] = jnp.where(own == k, m[:half_lev], m[half_lev:])
                v = flux[:half_lev]
                c0 = jnp.sum((u + v) * one, axis=1, keepdims=True)
                c1 = jnp.sum((u - v) * cos, axis=1, keepdims=True)
                s1 = jnp.sum((u - v) * sin, axis=1, keepdims=True)
                at = KF % LANE
                lanes = slice(half - LANE, half)
                spot = slice(t * half_lev, (t + 1) * half_lev)
                target[spot, lanes] = jnp.where(
                    lane == at, c0, jnp.where(lane == at + 1, c1, jnp.where(lane == at + 2, s1, target[spot, lanes]))
                )


def third_kernel(lat_count, local, recv, after, fwd, turn, keep, send, block):
    tracers, levels, cols = recv.shape
    south, polar, _ = latitude_role(lat_count)
    lon, own, _ = longitude_role()
    half_lev = levels // 2
    n_half = tracers * half_lev
    half = fwd.shape[-1] // 2

    @pl.when(polar)
    def _():
        sign = jnp.where(south, -1.0, 1.0).astype(jnp.float32)
        block[...] = local[...]
        for t in range(tracers):
            m = recv[t] * sign
            for k in (0, 1):
                first = k * n_half + t * half_lev
                block[first : first + half_lev, :cols] += jnp.where(own == k, m[:half_lev], m[half_lev:])
        c, s = turned(dot3(block[...], fwd), turn, lon)
        keep[:, :half], keep[:, half:] = c[:n_half], s[:n_half]
        send[:, :half], send[:, half:] = c[n_half:], s[n_half:]


def token_kernel(x, *rest):
    rest[-1][...] = x[:8, :LANE]


def sum_kernel(lat_count, mine, got, after, out):
    _, polar, _ = latitude_role(lat_count)

    @pl.when(polar)
    def _():
        out[...] = mine[...] + got[...]

    @pl.when(jnp.logical_not(polar))
    def _():
        out[:8] = got[:8]


def total_kernel(lat_count, mine, across, after, out):
    _, polar, _ = latitude_role(lat_count)

    @pl.when(polar)
    def _():
        out[...] = mine[...] + across[...]


def place(rows_ref, k, y, cols, half_lev):
    y = y.reshape(2, -1, half_lev, y.shape[-1])
    for h in (0, 1):
        rows_ref[k, :, h * half_lev : (h + 1) * half_lev, :] = y[h][..., :cols]


def cap_kernel(lat_count, circle, weights, mine, other, third, bwd, pole, out):
    _, tracers, levels, cols = out.shape
    half_lev = levels // 2
    n_half = tracers * half_lev
    half = bwd.shape[1] // 2
    _, polar, _ = latitude_role(lat_count)
    lon, own, _ = longitude_role()

    @pl.when(polar)
    def _():
        parts = (mine, own), (other, 1 - own)
        cos, sin = pole[lon, 1:2], pole[lon, 2:3]
        at = KF % LANE
        for source, h in parts:
            lev = pl.ds(pl.multiple_of(h * half_lev, half_lev), half_lev)
            for t in range(tracers):
                p = source[t * half_lev : (t + 1) * half_lev, half - LANE : half]
                c0, c1, s1 = p[:, at : at + 1], p[:, at + 1 : at + 2], p[:, at + 2 : at + 3]
                y = (1.0 / circle) * c0 + (2.0 / circle) * (c1 * cos + s1 * sin)
                out[0, t, lev, :] = y[:, :cols]
        blocks = [
            weighted(source[slot * n_half : (slot + 1) * n_half], weights[slot]) for slot in range(2) for source, _ in parts
        ]
        blocks.append(weighted(third[...], weights[2]))
        y = dot3(jnp.concatenate(blocks), bwd)
        places = [(slot + 1, h) for slot in range(2) for _, h in parts] + [(3, own)]
        for k, (slot, h) in enumerate(places):
            lev = pl.ds(pl.multiple_of(h * half_lev, half_lev), half_lev)
            out[slot, :, lev, :] = y[k * n_half : (k + 1) * n_half, :cols].reshape(tracers, half_lev, cols)


def finish_kernel(
    lat_count, circle, weights, caps, base, recv_a, recv_b, from_core, from_x, third, bwd, out, rows_ref, last_ref, sems,
):
    rows, tracers, levels, cols = base.shape
    half_lev = levels // 2
    south, polar, even = latitude_role(lat_count)
    _, own, right_core = longitude_role()

    @pl.when(polar)
    def _():
        copies = []
        for near in range(rows - 1):
            row = jnp.where(south, rows - 1 - near, near)
            copies.append(pltpu.make_async_copy(caps.at[near], out.at[row], sems.at[near]))
            copies[-1].start()
        row = jnp.where(south, 0, rows - 1)
        here, there = (pl.ds(pl.multiple_of(h * half_lev, half_lev), half_lev) for h in (own, 1 - own))
        copies.append(pltpu.make_async_copy(caps.at[rows - 1, :, here, :], out.at[row, :, here, :], sems.at[rows - 1]))
        copies[-1].start()
        y = dot3(weighted(third[...], weights[2]), bwd)
        last_ref[...] = y[:, :cols].reshape(tracers, half_lev, cols)
        copies.append(pltpu.make_async_copy(last_ref, out.at[row, :, there, :], sems.at[rows]))
        copies[-1].start()
        for copy in copies:
            copy.wait()

    @pl.when(jnp.logical_not(polar))
    def _():
        row = lax.broadcasted_iota(jnp.int32, (8, LANE), 0)
        lane = lax.broadcasted_iota(jnp.int32, (8, LANE), 1)
        start = cols // LANE * LANE
        low = jnp.where((row == 1) & (lane == 0), 1.0, 0.0).astype(jnp.float32)
        high = jnp.where((row == 0) & (lane == cols - 1 - start), 1.0, 0.0).astype(jnp.float32)
        dims = (((0,), (0,)), ((), ()))
        exact = lax.Precision.HIGHEST
        count = rows * tracers * levels
        core_side, x_side = from_core[:8, :count], from_x[:8, :count]
        left = jnp.where(right_core, x_side, core_side)
        right = jnp.where(right_core, core_side, x_side)
        first = lax.dot_general(left, low, dims, precision=exact, preferred_element_type=jnp.float32)
        end = lax.dot_general(right, high, dims, precision=exact, preferred_element_type=jnp.float32)
        shape = (rows, tracers, levels, LANE)
        first, end = first.reshape(shape), end.reshape(shape)
        side_a = recv_a[...]
        side_b = recv_b[...]
        copies = []
        for r in range(rows):
            value = base[r]
            if r == rows - 1:
                value = value + jnp.where(even, side_a, side_b)
            if r == 0:
                value = value - jnp.where(even, side_b, side_a)
            rows_ref[r] = value
            rows_ref[r, :, :, :LANE] -= first[r]
            rows_ref[r, :, :, start:] += end[r][..., : cols - start]
            copies.append(pltpu.make_async_copy(rows_ref.at[r], out.at[r], sems.at[r]))
            copies[-1].start()
        for copy in copies:
            copy.wait()


def fast_body(adj, east, north, cutoff):
    lat_count, lon_count = lax.axis_size("lat"), lax.axis_size("lon")
    rows, tracers, levels, cols = adj.shape
    circle = cols * lon_count
    fwd, bwd, turn, pole = tables(cols, circle, lon_count)
    wide, width = fwd.shape[1:]
    last = lat_count - 1
    f32 = jnp.float32
    params = pltpu.CompilerParams(vmem_limit_bytes=40 << 20)
    dma = pltpu.SemaphoreType.DMA
    vmem = pl.BlockSpec(memory_space=VMEM)
    smem = pl.BlockSpec(memory_space=pltpu.SMEM)
    anywhere = pl.BlockSpec(memory_space=pl.ANY)
    far = pl.BlockSpec(memory_space=HBM)
    n_half = tracers * levels // 2
    pair, single = (2 * n_half, width), (n_half, width)

    def put(x, space):
        return pltpu.with_memory_space_constraint(x, space)

    def call(kernel, outs, *args, scratch=(), cost=LIGHT):
        return pl.pallas_call(
            functools.partial(kernel, lat_count),
            out_shape=[VMEM(s, f32) for s in outs],
            in_specs=[vmem] * len(args),
            out_specs=[vmem] * len(outs),
            scratch_shapes=[VMEM(s, f32) for s in scratch],
            compiler_params=params,
            cost_estimate=cost,
        )(*(put(x, VMEM) for x in args))

    lats, lons = range(lat_count), range(lon_count)

    def swap(x, pairs):
        return lax.ppermute(x, ("lat", "lon"), [(a * lon_count + i, b * lon_count + j) for a, i, b, j in pairs])

    by_core = [(a, i, a, i ^ 1) for a in lats for i in lons]
    by_x = [(a, i, a, i ^ 2) for a in lats for i in lons]
    by_lat = [(a, i, a ^ 1, i) for a in lats for i in lons]
    by_next = [(a, i, ((a + 1) ^ 1) - 1, i) for a in range(1, last) for i in lons]

    edge = pl.pallas_call(
        functools.partial(edge_kernel, lat_count),
        out_shape=VMEM(adj.shape[1:], f32),
        in_specs=[far] * 2,
        out_specs=vmem,
        scratch_shapes=[VMEM(adj.shape[1:], f32), VMEM(north.shape[1:], f32), dma((2,))],
        cost_estimate=HEAVY,
        compiler_params=params,
    )(put(adj, HBM), put(north, HBM))
    recv_a = swap(edge, by_lat)
    base, edge_b, keep, send, local = call(
        local_kernel,
        (adj.shape, adj.shape[1:], pair, pair, (2 * n_half, wide)),
        edge,
        adj,
        east,
        north,
        fwd,
        turn,
        pole,
        scratch=((levels, wide), (rows, 2, tracers, levels // 2, wide), (rows, tracers, levels, LANE)),
    )
    got = swap(send, by_core)
    def token(*args):
        return pl.pallas_call(
            token_kernel,
            out_shape=VMEM((8, LANE), f32),
            in_specs=[vmem] * len(args),
            out_specs=vmem,
            compiler_params=params,
            cost_estimate=HEAVY,
        )(*(put(x, VMEM) for x in args))

    weights = pl.pallas_call(
        functools.partial(weight_kernel, lat_count, circle),
        out_shape=VMEM((rows - 1, 2, width // 2), f32),
        in_specs=[smem] + [vmem] * 2,
        out_specs=vmem,
        compiler_params=params,
        cost_estimate=HEAVY,
    )(cutoff, put(local, VMEM), put(turn, VMEM))
    (part,) = call(sum_kernel, (pair,), keep, got, weights)
    across = swap(part, by_x)
    recv_b = swap(edge_b, by_next)
    keep3, send3 = call(third_kernel, (single, single), local, recv_a, part, fwd, turn, scratch=((2 * n_half, wide),))
    got3 = swap(send3, by_core)
    (part3,) = call(sum_kernel, (single,), keep3, got3, send3)
    across3 = swap(part3, by_x)
    (mine,) = call(total_kernel, (pair,), part, across, part3)
    other = swap(mine, by_core)
    (mine3,) = call(total_kernel, (single,), part3, across3, token(part3, across, recv_b))
    other3 = swap(mine3, by_core)
    caps = pl.pallas_call(
        functools.partial(cap_kernel, lat_count, circle),
        out_shape=VMEM(adj.shape, f32),
        in_specs=[vmem] * 6,
        out_specs=vmem,
        compiler_params=params,
    )(*(put(x, VMEM) for x in (weights, mine, other, mine3, bwd, pole)))
    return pl.pallas_call(
        functools.partial(finish_kernel, lat_count, circle),
        out_shape=jax.ShapeDtypeStruct(adj.shape, f32),
        in_specs=[vmem] * 9,
        out_specs=anywhere,
        scratch_shapes=[VMEM(adj.shape, f32), VMEM((tracers, levels // 2, cols), f32), dma((rows + 1,))],
        compiler_params=params,
    )(*(put(x, VMEM) for x in (weights, caps, base, recv_a, recv_b, got, across, other3, bwd)))


full_precision = lax.Precision.HIGHEST


def extended(block, sides, width, periodic):
    for axis, dim in sides:
        count = lax.axis_size(axis)
        forward = [(i, i + 1) for i in range(count - 1)]
        if periodic:
            forward.append((count - 1, 0))
        backward = [(target, source) for source, target in forward]
        low = lax.ppermute(
            lax.slice_in_dim(block, block.shape[dim] - width, None, axis=dim), axis, forward
        )
        high = lax.ppermute(lax.slice_in_dim(block, 0, width, axis=dim), axis, backward)
        block = jnp.concatenate([low, block, high], axis=dim)
    return block


def from_partner(block, axis, stride):
    count = lax.axis_size(axis)
    route = []
    for low in range(count):
        high = low | 1 << stride
        if high != low and high < count:
            route += [(low, high), (high, low)]
    return lax.ppermute(block, axis, route)


def mode_table(columns, modes_kept, circle):
    wavenumber = jnp.arange(modes_kept, dtype=jnp.int32)
    product = columns[:, None] * wavenumber[None, :] % circle
    phases = product.astype(jnp.float32) * (2.0 * math.pi / circle)
    return jnp.concatenate([jnp.cos(phases), jnp.sin(phases)], axis=1)


def spectral_weights(latitude, cutoff, modes_kept, circle, total_lat):
    cap_lat = cutoff.shape[1]
    offsets = jnp.arange(cap_lat, dtype=jnp.int32)
    north_hit = latitude[..., None] == offsets
    south_hit = latitude[..., None] == total_lat - cap_lat + offsets
    chosen = jnp.sum(
        jnp.where(north_hit, cutoff[0], 0) + jnp.where(south_hit, cutoff[1], 0), axis=-1
    )
    wavenumber = jnp.arange(2 * modes_kept, dtype=jnp.int32) % modes_kept
    mode_weight = jnp.where(wavenumber == 0, 1.0, 2.0) / circle
    kept_mask = wavenumber <= chosen[..., None]
    return jnp.where(kept_mask, mode_weight, 0.0).astype(jnp.float32)


def general_body(adj_next, east_courant, north_courant, cutoff):
    lat_count = lax.axis_size("lat")
    lon_count = lax.axis_size("lon")
    lat_index = lax.axis_index("lat")
    lon_index = lax.axis_index("lon")
    lat_rows, tracers, levels, lon_cols = adj_next.shape
    circle = lon_cols * lon_count
    total_lat = lat_rows * lat_count
    modes_kept = KF
    cap_lat = cutoff.shape[1]
    zonal_flux = east_courant[:, None] * adj_next
    meridional = north_courant[:, None] * adj_next
    lon_padded = extended(zonal_flux, (("lon", 3),), 1, True)
    result = adj_next + lon_padded[..., 2:] - lon_padded[..., :-2]
    lat_padded = extended(meridional, (("lat", 0),), 1, False)
    result = result + lat_padded[2:] - lat_padded[:-2]
    edge_row = jnp.where(lat_index == 0, meridional[0], meridional[-1])
    pole_bit = lon_count.bit_length() - 2
    partner = from_partner(edge_row, "lon", pole_bit)
    north_sign = jnp.where(lat_index == 0, 1.0, 0.0).astype(jnp.float32)
    south_sign = jnp.where(lat_index == lat_count - 1, -1.0, 0.0).astype(jnp.float32)
    result = result.at[0].add(north_sign * partner)
    result = result.at[-1].add(south_sign * partner)
    latitude = lat_index * lat_rows + jnp.arange(lat_rows, dtype=jnp.int32)
    in_cap = (latitude < cap_lat) | (latitude >= total_lat - cap_lat)
    local_cols = lon_index * lon_cols + jnp.arange(lon_cols, dtype=jnp.int32)
    local_table = mode_table(local_cols, modes_kept, circle)
    weights = spectral_weights(latitude, cutoff, modes_kept, circle, total_lat)
    partial_sum = jnp.einsum(
        "acvn,nk->acvk",
        result,
        local_table,
        precision=full_precision,
        preferred_element_type=jnp.float32,
    )
    level_share = lax.psum_scatter(partial_sum, "lon", scatter_dimension=2, tiled=True)
    level_share = level_share * weights[:, None, None, :]
    totals = lax.all_gather(level_share, "lon", axis=2, tiled=True)
    rebuilt = jnp.einsum(
        "acvk,nk->acvn",
        totals,
        local_table,
        precision=full_precision,
        preferred_element_type=jnp.float32,
    )
    output = jnp.where(in_cap[:, None, None, None], rebuilt, result)
    return output


def body(adj, east, north, cutoff):
    lat_count, lon_count = lax.axis_size("lat"), lax.axis_size("lon")
    one_band = cutoff.shape[1] == adj.shape[0] == 4
    if one_band and lon_count == 4 and lat_count % 2 == 0 and lat_count >= 4 and adj.shape[2] % 16 == 0:
        return fast_body(adj, east, north, cutoff)
    return general_body(adj, east, north, cutoff)


def solution(mesh):
    return jax.shard_map(
        body,
        mesh=mesh,
        in_specs=(P("lat", None, None, "lon"), P("lat", None, "lon"), P("lat", None, "lon"), P()),
        out_specs=P("lat", None, None, "lon"),
        check_vma=False,
    )
```

```python
import functools
import math

import jax
import jax.numpy as jnp
import ml_dtypes
import numpy as np
from jax import lax
from jax.experimental import pallas as pl
from jax.experimental.pallas import tpu as pltpu
from jax.sharding import PartitionSpec as P

KF = 352
LANE = 128
VMEM = pltpu.VMEM
HBM = pltpu.HBM
HEAVY = pl.CostEstimate(flops=2**37, bytes_accessed=0, transcendentals=0)
LIGHT = pl.CostEstimate(flops=0, bytes_accessed=1000, transcendentals=0)


def ceil_to(value, unit):
    return -(-value // unit) * unit


def split16(table):
    high = table.astype(ml_dtypes.bfloat16)
    low = (table - high.astype(np.float64)).astype(ml_dtypes.bfloat16)
    return np.stack([high, low])


def tables(cols, circle, lon_count):
    wide = ceil_to(cols + 2, LANE)
    half = ceil_to(KF + 2, LANE)
    place = np.zeros(wide, np.int64)
    place[: cols + 1] = np.arange(cols + 1)
    place[-1] = -1
    live = np.zeros(wide)
    live[: cols + 1] = 1
    live[-1] = 1
    mode = np.arange(KF)
    phase = 2 * np.pi * ((place[:, None] * mode[None]) % circle) / circle
    forward = np.zeros((wide, 2 * half))
    forward[:, :KF] = np.cos(phase) * live[:, None]
    forward[:, half : half + KF] = np.sin(phase) * live[:, None]
    backward = forward.T.copy()
    backward[:, cols:] = 0
    turn = np.zeros((lon_count, 2, half), np.float32)
    angle = 2 * np.pi * ((np.arange(lon_count)[:, None] * mode[None]) % lon_count) / lon_count
    turn[:, 0, :KF] = np.cos(angle)
    turn[:, 1, :KF] = np.sin(angle)
    pole = np.zeros((lon_count, 4, wide), np.float32)
    for index in range(lon_count):
        first = 2 * np.pi * (place + index * cols) / circle
        pole[index, 0] = live
        pole[index, 1] = np.cos(first) * live
        pole[index, 2] = np.sin(first) * live
    return split16(forward), split16(backward), turn, pole


def dot3(block, table_ref):
    rows = block.shape[0]
    high = block.astype(jnp.bfloat16)
    low = (block - high.astype(jnp.float32)).astype(jnp.bfloat16)
    stack = jnp.dot(jnp.concatenate([high, low]), table_ref[0], preferred_element_type=jnp.float32)
    return stack[:rows] + stack[rows:] + jnp.dot(high, table_ref[1], preferred_element_type=jnp.float32)


def latitude_role(lat_count):
    lat = lax.axis_index("lat")
    south = lat == lat_count - 1
    return south, jnp.logical_or(lat == 0, south), lax.rem(lat, 2) == 0


def longitude_role():
    lon = lax.axis_index("lon")
    core = lax.rem(lon, 2)
    return lon, core, core == 0


def turned(p, turn, lon):
    half = p.shape[1] // 2
    a, b = turn[lon, 0:1], turn[lon, 1:2]
    c, s = p[:, :half], p[:, half:]
    return c * a - s * b, s * a + c * b


def weighted(block, weights):
    half = block.shape[1] // 2
    c, s = block[:, :half], block[:, half:]
    return jnp.concatenate([c * weights[0:1] + s * weights[1:2], s * weights[0:1] - c * weights[1:2]], axis=1)


def side_kernel(lat_count, circle, cutoff, after, adj, east, north, turn, pole, out, third, flux):
    rows, tracers, levels, cols = adj.shape
    wide = third.shape[1]
    half_lev = levels // 2
    n_half = tracers * half_lev
    south, polar, _ = latitude_role(lat_count)
    lon, own, _ = longitude_role()
    wave = lax.broadcasted_iota(jnp.int32, (1, turn.shape[-1]), 1)

    @pl.when(polar)
    def _():
        for slot in range(rows - 1):
            row = jnp.where(south, rows - 2 - slot, slot + 1)
            kept = jnp.where(south, cutoff[1, row], cutoff[0, row])
            weight = jnp.where(wave <= kept, jnp.where(wave == 0, 1.0 / circle, 2.0 / circle), 0.0).astype(jnp.float32)
            for k in (0, 1):
                out[slot, k : k + 1] = weight * turn[lon, k : k + 1]
        sign = jnp.where(south, -1.0, 1.0).astype(jnp.float32)
        top, below = jnp.where(south, rows - 1, 0), jnp.where(south, rows - 2, 1)
        last, above = jnp.where(south, 0, rows - 1), jnp.where(south, 1, rows - 2)
        flux[..., cols:] = jnp.zeros(flux.shape[:-1] + (wide - cols,), jnp.float32)
        one, cos, sin = (pole[lon, k : k + 1] for k in range(3))
        spare = (cols + 2) // LANE * LANE
        at = cols + 2 - spare
        lane = lax.broadcasted_iota(jnp.int32, (levels, wide - spare), 1)
        for t in range(tracers):
            flux[0, t, :, :cols] = east[top] * adj[top, t]
            flux[1, t, :, :cols] = east[last] * adj[last, t]
            flux[2, t, :, :cols] = adj[top, t] + sign * (north[below] * adj[below, t])
            flux[3, t, :, :cols] = sign * (north[top] * adj[top, t])
            f = flux[0, t]
            u = pltpu.roll(f, wide - 1, 1) - pltpu.roll(f, 1, 1) + flux[2, t]
            v = flux[3, t]
            c0 = jnp.sum((u + v) * one, axis=1, keepdims=True)
            c1 = jnp.sum((u - v) * cos, axis=1, keepdims=True)
            s1 = jnp.sum((u - v) * sin, axis=1, keepdims=True)
            f = flux[1, t]
            move = pltpu.roll(f, wide - 1, 1) - pltpu.roll(f, 1, 1)
            inner = adj[last, t] - sign * (north[above] * adj[above, t]) + move[:, :cols]
            tail = jnp.where(lane == at, c0, jnp.where(lane == at + 1, c1, jnp.where(lane == at + 2, s1, move[:, spare:])))
            for k in (0, 1):
                spot = slice(k * n_half + t * half_lev, k * n_half + (t + 1) * half_lev)
                first, second = slice(0, half_lev), slice(half_lev, levels)
                third[spot, spare:] = jnp.where(own == k, tail[first], tail[second])
                third[spot, :cols] = jnp.where(own == k, inner[first], inner[second])


def edge_kernel(lat_count, adj_hbm, north_hbm, edge, adj, north, sems):
    _, _, even = latitude_role(lat_count)
    row = jnp.where(even, adj_hbm.shape[0] - 1, 0)
    copies = (
        pltpu.make_async_copy(adj_hbm.at[row], adj, sems.at[0]),
        pltpu.make_async_copy(north_hbm.at[row], north, sems.at[1]),
    )
    for copy in copies:
        copy.start()
    for copy in copies:
        copy.wait()
    edge[...] = north[...][None] * adj[...]


def local_kernel(
    lat_count, after, adj, east, north, fwd, turn, base, edge, keep, send, flux, wide_x, ends
):
    rows, tracers, levels, cols = adj.shape
    wide = flux.shape[-1]
    south, polar, even = latitude_role(lat_count)
    lon, own, _ = longitude_role()
    half_lev = levels // 2
    n_half = tracers * half_lev
    half = fwd.shape[-1] // 2
    row_b = jnp.where(even, 0, rows - 1)
    flux[:, cols:] = jnp.zeros((levels, wide - cols), jnp.float32)

    def transported(r, t):
        out = adj[r, t]
        if r + 1 < rows:
            out = out + north[r + 1] * adj[r + 1, t]
        if r > 0:
            out = out - north[r - 1] * adj[r - 1, t]
        return out

    def spread(r, t):
        flux[:, :cols] = east[r] * adj[r, t]
        f = flux[...]
        return pltpu.roll(f, wide - 1, 1) - pltpu.roll(f, 1, 1), f

    @pl.when(jnp.logical_not(polar))
    def _():
        start = cols // LANE * LANE
        lane = lax.broadcasted_iota(jnp.int32, (levels, LANE), 1)
        at = cols - 1 - start
        for r in range(rows):
            for t in range(tracers):
                move, f = spread(r, t)
                base[r, t] = transported(r, t) + move[:, :cols]
                ends[r, t] = jnp.where(lane == 0, f[:, :LANE], jnp.where(lane == at, f[:, start : start + LANE], 0.0))
        row = lax.broadcasted_iota(jnp.int32, (8, LANE), 0)
        lane = lax.broadcasted_iota(jnp.int32, (8, LANE), 1)
        pick = jnp.where((row == 0) & (lane == 0) | (row == 1) & (lane == at), 1.0, 0.0).astype(jnp.float32)
        sides = lax.dot_general(
            pick,
            ends[...].reshape(rows * tracers * levels, LANE),
            (((1,), (1,)), ((), ())),
            precision=lax.Precision.HIGHEST,
            preferred_element_type=jnp.float32,
        )
        send[:8, : sides.shape[1]] = sides
        edge[...] = north[row_b][None] * adj[row_b]

    @pl.when(polar)
    def _():
        for r in range(1, rows - 1):
            slot = jnp.where(south, rows - 2 - r, r - 1)
            for t in range(tracers):
                move, _ = spread(r, t)
                inner = transported(r, t) + move[:, :cols]
                for h in (0, 1):
                    part = slice(h * half_lev, (h + 1) * half_lev)
                    where = jnp.where(own == h, 0, 1)
                    wide_x[slot, where, t, :, :cols] = inner[part]
                    wide_x[slot, where, t, :, cols:] = move[part, cols:]
        c, s = turned(dot3(wide_x[...].reshape(4 * n_half, wide), fwd), turn, lon)
        for slot in range(2):
            spot = slice(slot * n_half, (slot + 1) * n_half)
            first = slice(2 * slot * n_half, (2 * slot + 1) * n_half)
            second = slice((2 * slot + 1) * n_half, (2 * slot + 2) * n_half)
            keep[spot, :half], keep[spot, half:] = c[first], s[first]
            send[spot, :half], send[spot, half:] = c[second], s[second]


def third_kernel(lat_count, local, recv, after, fwd, turn, keep, send, block):
    tracers, levels, cols = recv.shape
    south, polar, _ = latitude_role(lat_count)
    lon, own, _ = longitude_role()
    half_lev = levels // 2
    n_half = tracers * half_lev
    half = fwd.shape[-1] // 2

    @pl.when(polar)
    def _():
        sign = jnp.where(south, -1.0, 1.0).astype(jnp.float32)
        block[...] = local[...]
        for t in range(tracers):
            m = recv[t] * sign
            for k in (0, 1):
                first = k * n_half + t * half_lev
                block[first : first + half_lev, :cols] += jnp.where(own == k, m[:half_lev], m[half_lev:])
        c, s = turned(dot3(block[...], fwd), turn, lon)
        keep[:, :half], keep[:, half:] = c[:n_half], s[:n_half]
        send[:, :half], send[:, half:] = c[n_half:], s[n_half:]
        at = KF % LANE
        spare = (cols + 2) // LANE * LANE
        lane = lax.broadcasted_iota(jnp.int32, (2 * n_half, LANE), 1)
        sums = pltpu.roll(local[:, spare : spare + LANE], (at - (cols + 2)) % LANE, 1)
        sums = jnp.where((lane >= at) & (lane < at + 3), sums, 0.0)
        keep[:, half - LANE : half] += sums[:n_half]
        send[:, half - LANE : half] += sums[n_half:]


def token_kernel(x, *rest):
    rest[-1][...] = x[:8, :LANE]


def sum_kernel(lat_count, mine, got, after, out):
    _, polar, _ = latitude_role(lat_count)

    @pl.when(polar)
    def _():
        out[...] = mine[...] + got[...]

    @pl.when(jnp.logical_not(polar))
    def _():
        out[:8] = got[:8]


def total_kernel(lat_count, mine, across, after, out):
    _, polar, _ = latitude_role(lat_count)

    @pl.when(polar)
    def _():
        out[...] = mine[...] + across[...]


def place(rows_ref, k, y, cols, half_lev):
    y = y.reshape(2, -1, half_lev, y.shape[-1])
    for h in (0, 1):
        rows_ref[k, :, h * half_lev : (h + 1) * half_lev, :] = y[h][..., :cols]


def pole_row(sums, t, half_lev, half, pole, lon, circle):
    p = sums[t * half_lev : (t + 1) * half_lev, half - LANE : half]
    at = KF % LANE
    c0, c1, s1 = p[:, at : at + 1], p[:, at + 1 : at + 2], p[:, at + 2 : at + 3]
    return (1.0 / circle) * c0 + (2.0 / circle) * (c1 * pole[lon, 1:2] + s1 * pole[lon, 2:3])


def cap_kernel(lat_count, circle, weights, mine, other, third, bwd, pole, out):
    _, tracers, levels, cols = out.shape
    half_lev = levels // 2
    n_half = tracers * half_lev
    half = bwd.shape[1] // 2
    _, polar, _ = latitude_role(lat_count)
    lon, own, _ = longitude_role()

    @pl.when(polar)
    def _():
        parts = (mine, own), (other, 1 - own)
        lev = pl.ds(pl.multiple_of(own * half_lev, half_lev), half_lev)
        for t in range(tracers):
            out[0, t, lev, :] = pole_row(third, t, half_lev, half, pole, lon, circle)[:, :cols]
        blocks = [
            weighted(source[slot * n_half : (slot + 1) * n_half], weights[slot]) for slot in range(2) for source, _ in parts
        ]
        blocks.append(weighted(third[...], weights[2]))
        y = dot3(jnp.concatenate(blocks), bwd)
        places = [(slot + 1, h) for slot in range(2) for _, h in parts] + [(3, own)]
        for k, (slot, h) in enumerate(places):
            lev = pl.ds(pl.multiple_of(h * half_lev, half_lev), half_lev)
            out[slot, :, lev, :] = y[k * n_half : (k + 1) * n_half, :cols].reshape(tracers, half_lev, cols)


def finish_kernel(
    lat_count, circle, weights, caps, base, recv_a, recv_b, from_core, from_x, third, bwd, pole, out, rows_ref, last_ref, pole_ref,
    sems,
):
    rows, tracers, levels, cols = base.shape
    half_lev = levels // 2
    south, polar, even = latitude_role(lat_count)
    lon, own, right_core = longitude_role()

    @pl.when(polar)
    def _():
        here, there = (pl.ds(pl.multiple_of(h * half_lev, half_lev), half_lev) for h in (own, 1 - own))
        top, row = jnp.where(south, rows - 1, 0), jnp.where(south, 0, rows - 1)
        moves = [(caps.at[near], out.at[jnp.where(south, rows - 1 - near, near)]) for near in range(1, rows - 1)]
        moves += [(caps.at[near, :, here, :], out.at[at, :, here, :]) for near, at in ((0, top), (rows - 1, row))]
        copies = []
        for k, (source, target) in enumerate(moves):
            copies.append(pltpu.make_async_copy(source, target, sems.at[k]))
            copies[-1].start()
        for t in range(tracers):
            pole_ref[t] = pole_row(third, t, half_lev, bwd.shape[1] // 2, pole, lon, circle)[:, :cols]
        copies.append(pltpu.make_async_copy(pole_ref, out.at[top, :, there, :], sems.at[rows + 1]))
        copies[-1].start()
        y = dot3(weighted(third[...], weights[2]), bwd)
        last_ref[...] = y[:, :cols].reshape(tracers, half_lev, cols)
        copies.append(pltpu.make_async_copy(last_ref, out.at[row, :, there, :], sems.at[rows]))
        copies[-1].start()
        for copy in copies:
            copy.wait()

    @pl.when(jnp.logical_not(polar))
    def _():
        row = lax.broadcasted_iota(jnp.int32, (8, LANE), 0)
        lane = lax.broadcasted_iota(jnp.int32, (8, LANE), 1)
        start = cols // LANE * LANE
        low = jnp.where((row == 1) & (lane == 0), 1.0, 0.0).astype(jnp.float32)
        high = jnp.where((row == 0) & (lane == cols - 1 - start), 1.0, 0.0).astype(jnp.float32)
        dims = (((0,), (0,)), ((), ()))
        exact = lax.Precision.HIGHEST
        count = rows * tracers * levels
        core_side, x_side = from_core[:8, :count], from_x[:8, :count]
        left = jnp.where(right_core, x_side, core_side)
        right = jnp.where(right_core, core_side, x_side)
        first = lax.dot_general(left, low, dims, precision=exact, preferred_element_type=jnp.float32)
        end = lax.dot_general(right, high, dims, precision=exact, preferred_element_type=jnp.float32)
        shape = (rows, tracers, levels, LANE)
        first, end = first.reshape(shape), end.reshape(shape)
        side_a = recv_a[...]
        side_b = recv_b[...]
        copies = []
        for r in range(rows):
            value = base[r]
            if r == rows - 1:
                value = value + jnp.where(even, side_a, side_b)
            if r == 0:
                value = value - jnp.where(even, side_b, side_a)
            rows_ref[r] = value
            rows_ref[r, :, :, :LANE] -= first[r]
            rows_ref[r, :, :, start:] += end[r][..., : cols - start]
            copies.append(pltpu.make_async_copy(rows_ref.at[r], out.at[r], sems.at[r]))
            copies[-1].start()
        for copy in copies:
            copy.wait()


def fast_body(adj, east, north, cutoff):
    lat_count, lon_count = lax.axis_size("lat"), lax.axis_size("lon")
    rows, tracers, levels, cols = adj.shape
    circle = cols * lon_count
    fwd, bwd, turn, pole = tables(cols, circle, lon_count)
    wide, width = fwd.shape[1:]
    last = lat_count - 1
    f32 = jnp.float32
    params = pltpu.CompilerParams(vmem_limit_bytes=40 << 20)
    dma = pltpu.SemaphoreType.DMA
    vmem = pl.BlockSpec(memory_space=VMEM)
    smem = pl.BlockSpec(memory_space=pltpu.SMEM)
    anywhere = pl.BlockSpec(memory_space=pl.ANY)
    far = pl.BlockSpec(memory_space=HBM)
    n_half = tracers * levels // 2
    pair, single = (2 * n_half, width), (n_half, width)
    half_row = (tracers, levels // 2, cols)

    def put(x, space):
        return pltpu.with_memory_space_constraint(x, space)

    def call(kernel, outs, *args, scratch=(), cost=LIGHT):
        return pl.pallas_call(
            functools.partial(kernel, lat_count),
            out_shape=[VMEM(s, f32) for s in outs],
            in_specs=[vmem] * len(args),
            out_specs=[vmem] * len(outs),
            scratch_shapes=[VMEM(s, f32) for s in scratch],
            compiler_params=params,
            cost_estimate=cost,
        )(*(put(x, VMEM) for x in args))

    lats, lons = range(lat_count), range(lon_count)

    def swap(x, pairs):
        return lax.ppermute(x, ("lat", "lon"), [(a * lon_count + i, b * lon_count + j) for a, i, b, j in pairs])

    by_core = [(a, i, a, i ^ 1) for a in lats for i in lons]
    by_x = [(a, i, a, i ^ 2) for a in lats for i in lons]
    by_lat = [(a, i, a ^ 1, i) for a in lats for i in lons]
    by_next = [(a, i, ((a + 1) ^ 1) - 1, i) for a in range(1, last) for i in lons]

    edge = pl.pallas_call(
        functools.partial(edge_kernel, lat_count),
        out_shape=VMEM(adj.shape[1:], f32),
        in_specs=[far] * 2,
        out_specs=vmem,
        scratch_shapes=[VMEM(adj.shape[1:], f32), VMEM(north.shape[1:], f32), dma((2,))],
        cost_estimate=HEAVY,
        compiler_params=params,
    )(put(adj, HBM), put(north, HBM))
    recv_a = swap(edge, by_lat)
    base, edge_b, keep, send = call(
        local_kernel,
        (adj.shape, adj.shape[1:], pair, pair),
        edge,
        adj,
        east,
        north,
        fwd,
        turn,
        scratch=((levels, wide), (rows - 2, 2, tracers, levels // 2, wide), (rows, tracers, levels, LANE)),
    )

    def token(*args):
        return pl.pallas_call(
            token_kernel,
            out_shape=VMEM((8, LANE), f32),
            in_specs=[vmem] * len(args),
            out_specs=vmem,
            compiler_params=params,
            cost_estimate=HEAVY,
        )(*(put(x, VMEM) for x in args))

    got = swap(send, by_core)
    weights, local = pl.pallas_call(
        functools.partial(side_kernel, lat_count, circle),
        out_shape=[VMEM((rows - 1, 2, width // 2), f32), VMEM((2 * n_half, wide), f32)],
        in_specs=[smem] + [vmem] * 6,
        out_specs=[vmem] * 2,
        scratch_shapes=[VMEM((4, tracers, levels, wide), f32)],
        compiler_params=params,
        cost_estimate=HEAVY,
    )(cutoff, *(put(x, VMEM) for x in (keep, adj, east, north, turn, pole)))
    (part,) = call(sum_kernel, (pair,), keep, got, weights)
    across = swap(part, by_x)
    recv_b = swap(edge_b, by_next)
    keep3, send3 = call(third_kernel, (single, single), local, recv_a, part, fwd, turn, scratch=((2 * n_half, wide),))
    got3 = swap(send3, by_core)
    (part3,) = call(sum_kernel, (single,), keep3, got3, send3)
    across3 = swap(part3, by_x)
    (mine,) = call(total_kernel, (pair,), part, across, part3)
    other = swap(mine, by_core)
    (mine3,) = call(total_kernel, (single,), part3, across3, token(part3, across, recv_b))
    other3 = swap(mine3, by_core)
    caps = pl.pallas_call(
        functools.partial(cap_kernel, lat_count, circle),
        out_shape=VMEM(adj.shape, f32),
        in_specs=[vmem] * 6,
        out_specs=vmem,
        compiler_params=params,
    )(*(put(x, VMEM) for x in (weights, mine, other, mine3, bwd, pole)))
    return pl.pallas_call(
        functools.partial(finish_kernel, lat_count, circle),
        out_shape=jax.ShapeDtypeStruct(adj.shape, f32),
        in_specs=[vmem] * 10,
        out_specs=anywhere,
        scratch_shapes=[VMEM(adj.shape, f32), VMEM(half_row, f32), VMEM(half_row, f32), dma((rows + 2,))],
        compiler_params=params,
    )(*(put(x, VMEM) for x in (weights, caps, base, recv_a, recv_b, got, across, other3, bwd, pole)))


full_precision = lax.Precision.HIGHEST


def extended(block, sides, width, periodic):
    for axis, dim in sides:
        count = lax.axis_size(axis)
        forward = [(i, i + 1) for i in range(count - 1)]
        if periodic:
            forward.append((count - 1, 0))
        backward = [(target, source) for source, target in forward]
        low = lax.ppermute(
            lax.slice_in_dim(block, block.shape[dim] - width, None, axis=dim), axis, forward
        )
        high = lax.ppermute(lax.slice_in_dim(block, 0, width, axis=dim), axis, backward)
        block = jnp.concatenate([low, block, high], axis=dim)
    return block


def from_partner(block, axis, stride):
    count = lax.axis_size(axis)
    route = []
    for low in range(count):
        high = low | 1 << stride
        if high != low and high < count:
            route += [(low, high), (high, low)]
    return lax.ppermute(block, axis, route)


def mode_table(columns, modes_kept, circle):
    wavenumber = jnp.arange(modes_kept, dtype=jnp.int32)
    product = columns[:, None] * wavenumber[None, :] % circle
    phases = product.astype(jnp.float32) * (2.0 * math.pi / circle)
    return jnp.concatenate([jnp.cos(phases), jnp.sin(phases)], axis=1)


def spectral_weights(latitude, cutoff, modes_kept, circle, total_lat):
    cap_lat = cutoff.shape[1]
    offsets = jnp.arange(cap_lat, dtype=jnp.int32)
    north_hit = latitude[..., None] == offsets
    south_hit = latitude[..., None] == total_lat - cap_lat + offsets
    chosen = jnp.sum(
        jnp.where(north_hit, cutoff[0], 0) + jnp.where(south_hit, cutoff[1], 0), axis=-1
    )
    wavenumber = jnp.arange(2 * modes_kept, dtype=jnp.int32) % modes_kept
    mode_weight = jnp.where(wavenumber == 0, 1.0, 2.0) / circle
    kept_mask = wavenumber <= chosen[..., None]
    return jnp.where(kept_mask, mode_weight, 0.0).astype(jnp.float32)


def general_body(adj_next, east_courant, north_courant, cutoff):
    lat_count = lax.axis_size("lat")
    lon_count = lax.axis_size("lon")
    lat_index = lax.axis_index("lat")
    lon_index = lax.axis_index("lon")
    lat_rows, tracers, levels, lon_cols = adj_next.shape
    circle = lon_cols * lon_count
    total_lat = lat_rows * lat_count
    modes_kept = KF
    cap_lat = cutoff.shape[1]
    zonal_flux = east_courant[:, None] * adj_next
    meridional = north_courant[:, None] * adj_next
    lon_padded = extended(zonal_flux, (("lon", 3),), 1, True)
    result = adj_next + lon_padded[..., 2:] - lon_padded[..., :-2]
    lat_padded = extended(meridional, (("lat", 0),), 1, False)
    result = result + lat_padded[2:] - lat_padded[:-2]
    edge_row = jnp.where(lat_index == 0, meridional[0], meridional[-1])
    pole_bit = lon_count.bit_length() - 2
    partner = from_partner(edge_row, "lon", pole_bit)
    north_sign = jnp.where(lat_index == 0, 1.0, 0.0).astype(jnp.float32)
    south_sign = jnp.where(lat_index == lat_count - 1, -1.0, 0.0).astype(jnp.float32)
    result = result.at[0].add(north_sign * partner)
    result = result.at[-1].add(south_sign * partner)
    latitude = lat_index * lat_rows + jnp.arange(lat_rows, dtype=jnp.int32)
    in_cap = (latitude < cap_lat) | (latitude >= total_lat - cap_lat)
    local_cols = lon_index * lon_cols + jnp.arange(lon_cols, dtype=jnp.int32)
    local_table = mode_table(local_cols, modes_kept, circle)
    weights = spectral_weights(latitude, cutoff, modes_kept, circle, total_lat)
    partial_sum = jnp.einsum(
        "acvn,nk->acvk",
        result,
        local_table,
        precision=full_precision,
        preferred_element_type=jnp.float32,
    )
    level_share = lax.psum_scatter(partial_sum, "lon", scatter_dimension=2, tiled=True)
    level_share = level_share * weights[:, None, None, :]
    totals = lax.all_gather(level_share, "lon", axis=2, tiled=True)
    rebuilt = jnp.einsum(
        "acvk,nk->acvn",
        totals,
        local_table,
        precision=full_precision,
        preferred_element_type=jnp.float32,
    )
    output = jnp.where(in_cap[:, None, None, None], rebuilt, result)
    return output


def body(adj, east, north, cutoff):
    lat_count, lon_count = lax.axis_size("lat"), lax.axis_size("lon")
    one_band = cutoff.shape[1] == adj.shape[0] == 4
    if one_band and lon_count == 4 and lat_count % 2 == 0 and lat_count >= 4 and adj.shape[2] % 16 == 0:
        return fast_body(adj, east, north, cutoff)
    return general_body(adj, east, north, cutoff)


def solution(mesh):
    return jax.shard_map(
        body,
        mesh=mesh,
        in_specs=(P("lat", None, None, "lon"), P("lat", None, "lon"), P("lat", None, "lon"), P()),
        out_specs=P("lat", None, None, "lon"),
        check_vma=False,
    )
```

```python
import functools
import math

import jax
import jax.numpy as jnp
import ml_dtypes
import numpy as np
from jax import lax
from jax.experimental import pallas as pl
from jax.experimental.pallas import tpu as pltpu
from jax.sharding import PartitionSpec as P

KF = 352
LANE = 128
VMEM = pltpu.VMEM
HBM = pltpu.HBM
HEAVY = pl.CostEstimate(flops=2**37, bytes_accessed=0, transcendentals=0)
LIGHT = pl.CostEstimate(flops=0, bytes_accessed=1000, transcendentals=0)


def ceil_to(value, unit):
    return -(-value // unit) * unit


def split16(table):
    high = table.astype(ml_dtypes.bfloat16)
    low = (table - high.astype(np.float64)).astype(ml_dtypes.bfloat16)
    return np.stack([high, low])


def tables(cols, circle, lon_count):
    wide = ceil_to(cols + 2, LANE)
    half = ceil_to(KF + 2, LANE)
    place = np.zeros(wide, np.int64)
    place[: cols + 1] = np.arange(cols + 1)
    place[-1] = -1
    live = np.zeros(wide)
    live[: cols + 1] = 1
    live[-1] = 1
    mode = np.arange(KF)
    phase = 2 * np.pi * ((place[:, None] * mode[None]) % circle) / circle
    forward = np.zeros((wide, 2 * half))
    forward[:, :KF] = np.cos(phase) * live[:, None]
    forward[:, half : half + KF] = np.sin(phase) * live[:, None]
    backward = forward.T.copy()
    backward[:, cols:] = 0
    turn = np.zeros((lon_count, 2, half), np.float32)
    angle = 2 * np.pi * ((np.arange(lon_count)[:, None] * mode[None]) % lon_count) / lon_count
    turn[:, 0, :KF] = np.cos(angle)
    turn[:, 1, :KF] = np.sin(angle)
    pole = np.zeros((lon_count, 4, wide), np.float32)
    for index in range(lon_count):
        first = 2 * np.pi * (place + index * cols) / circle
        pole[index, 0] = live
        pole[index, 1] = np.cos(first) * live
        pole[index, 2] = np.sin(first) * live
    return split16(forward), split16(backward), turn, pole


def dot3(block, table_ref, first=0, count=None):
    rows = block.shape[0]
    count = table_ref.shape[2] if count is None else count
    high_table, low_table = (table_ref[k, :, first : first + count] for k in (0, 1))
    high = block.astype(jnp.bfloat16)
    low = (block - high.astype(jnp.float32)).astype(jnp.bfloat16)
    stack = jnp.dot(jnp.concatenate([high, low]), high_table, preferred_element_type=jnp.float32)
    return stack[:rows] + stack[rows:] + jnp.dot(high, low_table, preferred_element_type=jnp.float32)


def latitude_role(lat_count):
    lat = lax.axis_index("lat")
    south = lat == lat_count - 1
    return south, jnp.logical_or(lat == 0, south), lax.rem(lat, 2) == 0


def longitude_role():
    lon = lax.axis_index("lon")
    core = lax.rem(lon, 2)
    return lon, core, core == 0


def turned(p, turn, lon):
    half = p.shape[1] // 2
    a, b = turn[lon, 0:1], turn[lon, 1:2]
    c, s = p[:, :half], p[:, half:]
    return c * a - s * b, s * a + c * b


def weighted(block, weights):
    half = block.shape[1] // 2
    c, s = block[:, :half], block[:, half:]
    return jnp.concatenate([c * weights[0:1] + s * weights[1:2], s * weights[0:1] - c * weights[1:2]], axis=1)


def side_kernel(lat_count, circle, cutoff, after, adj, east, north, turn, pole, out, third, flux):
    rows, tracers, levels, cols = adj.shape
    wide = third.shape[1]
    half_lev = levels // 2
    n_half = tracers * half_lev
    south, polar, _ = latitude_role(lat_count)
    lon, own, _ = longitude_role()
    wave = lax.broadcasted_iota(jnp.int32, (1, turn.shape[-1]), 1)

    @pl.when(polar)
    def _():
        for slot in range(rows - 1):
            row = jnp.where(south, rows - 2 - slot, slot + 1)
            kept = jnp.where(south, cutoff[1, row], cutoff[0, row])
            weight = jnp.where(wave <= kept, jnp.where(wave == 0, 1.0 / circle, 2.0 / circle), 0.0).astype(jnp.float32)
            for k in (0, 1):
                out[slot, k : k + 1] = weight * turn[lon, k : k + 1]
        sign = jnp.where(south, -1.0, 1.0).astype(jnp.float32)
        top, below = jnp.where(south, rows - 1, 0), jnp.where(south, rows - 2, 1)
        last, above = jnp.where(south, 0, rows - 1), jnp.where(south, 1, rows - 2)
        flux[..., cols:] = jnp.zeros(flux.shape[:-1] + (wide - cols,), jnp.float32)
        one, cos, sin = (pole[lon, k : k + 1] for k in range(3))
        spare = (cols + 2) // LANE * LANE
        at = cols + 2 - spare
        lane = lax.broadcasted_iota(jnp.int32, (levels, wide - spare), 1)
        for t in range(tracers):
            flux[0, t, :, :cols] = east[top] * adj[top, t]
            flux[1, t, :, :cols] = east[last] * adj[last, t]
            flux[2, t, :, :cols] = adj[top, t] + sign * (north[below] * adj[below, t])
            flux[3, t, :, :cols] = sign * (north[top] * adj[top, t])
            f = flux[0, t]
            u = pltpu.roll(f, wide - 1, 1) - pltpu.roll(f, 1, 1) + flux[2, t]
            v = flux[3, t]
            c0 = jnp.sum((u + v) * one, axis=1, keepdims=True)
            c1 = jnp.sum((u - v) * cos, axis=1, keepdims=True)
            s1 = jnp.sum((u - v) * sin, axis=1, keepdims=True)
            f = flux[1, t]
            move = pltpu.roll(f, wide - 1, 1) - pltpu.roll(f, 1, 1)
            inner = adj[last, t] - sign * (north[above] * adj[above, t]) + move[:, :cols]
            tail = jnp.where(lane == at, c0, jnp.where(lane == at + 1, c1, jnp.where(lane == at + 2, s1, move[:, spare:])))
            for k in (0, 1):
                spot = slice(k * n_half + t * half_lev, k * n_half + (t + 1) * half_lev)
                first, second = slice(0, half_lev), slice(half_lev, levels)
                third[spot, spare:] = jnp.where(own == k, tail[first], tail[second])
                third[spot, :cols] = jnp.where(own == k, inner[first], inner[second])


def edge_kernel(lat_count, adj_hbm, north_hbm, edge, adj, north, sems):
    _, _, even = latitude_role(lat_count)
    row = jnp.where(even, adj_hbm.shape[0] - 1, 0)
    copies = (
        pltpu.make_async_copy(adj_hbm.at[row], adj, sems.at[0]),
        pltpu.make_async_copy(north_hbm.at[row], north, sems.at[1]),
    )
    for copy in copies:
        copy.start()
    for copy in copies:
        copy.wait()
    edge[...] = north[...][None] * adj[...]


def local_kernel(
    lat_count, after, adj, east, north, fwd, turn, base, edge, keep, send, flux, wide_x, ends
):
    rows, tracers, levels, cols = adj.shape
    wide = flux.shape[-1]
    south, polar, even = latitude_role(lat_count)
    lon, own, _ = longitude_role()
    half_lev = levels // 2
    n_half = tracers * half_lev
    half = fwd.shape[-1] // 2
    row_b = jnp.where(even, 0, rows - 1)
    flux[:, cols:] = jnp.zeros((levels, wide - cols), jnp.float32)

    def transported(r, t):
        out = adj[r, t]
        if r + 1 < rows:
            out = out + north[r + 1] * adj[r + 1, t]
        if r > 0:
            out = out - north[r - 1] * adj[r - 1, t]
        return out

    def spread(r, t):
        flux[:, :cols] = east[r] * adj[r, t]
        f = flux[...]
        return pltpu.roll(f, wide - 1, 1) - pltpu.roll(f, 1, 1), f

    @pl.when(jnp.logical_not(polar))
    def _():
        start = cols // LANE * LANE
        lane = lax.broadcasted_iota(jnp.int32, (levels, LANE), 1)
        at = cols - 1 - start
        for r in range(rows):
            for t in range(tracers):
                move, f = spread(r, t)
                base[r, t] = transported(r, t) + move[:, :cols]
                ends[r, t] = jnp.where(lane == 0, f[:, :LANE], jnp.where(lane == at, f[:, start : start + LANE], 0.0))
        row = lax.broadcasted_iota(jnp.int32, (8, LANE), 0)
        lane = lax.broadcasted_iota(jnp.int32, (8, LANE), 1)
        pick = jnp.where((row == 0) & (lane == 0) | (row == 1) & (lane == at), 1.0, 0.0).astype(jnp.float32)
        sides = lax.dot_general(
            pick,
            ends[...].reshape(rows * tracers * levels, LANE),
            (((1,), (1,)), ((), ())),
            precision=lax.Precision.HIGHEST,
            preferred_element_type=jnp.float32,
        )
        send[:8, : sides.shape[1]] = sides
        edge[...] = north[row_b][None] * adj[row_b]

    @pl.when(polar)
    def _():
        for r in range(1, rows - 1):
            slot = jnp.where(south, rows - 2 - r, r - 1)
            for t in range(tracers):
                move, _ = spread(r, t)
                inner = transported(r, t) + move[:, :cols]
                for h in (0, 1):
                    part = slice(h * half_lev, (h + 1) * half_lev)
                    where = jnp.where(own == h, 0, 1)
                    wide_x[slot, where, t, :, :cols] = inner[part]
                    wide_x[slot, where, t, :, cols:] = move[part, cols:]
        c, s = turned(dot3(wide_x[...].reshape(4 * n_half, wide), fwd), turn, lon)
        for slot in range(2):
            spot = slice(slot * n_half, (slot + 1) * n_half)
            first = slice(2 * slot * n_half, (2 * slot + 1) * n_half)
            second = slice((2 * slot + 1) * n_half, (2 * slot + 2) * n_half)
            keep[spot, :half], keep[spot, half:] = c[first], s[first]
            send[spot, :half], send[spot, half:] = c[second], s[second]


def third_kernel(lat_count, local, recv, after, fwd, turn, keep, send, block):
    tracers, levels, cols = recv.shape
    south, polar, _ = latitude_role(lat_count)
    lon, own, _ = longitude_role()
    half_lev = levels // 2
    n_half = tracers * half_lev
    half = fwd.shape[-1] // 2

    @pl.when(polar)
    def _():
        sign = jnp.where(south, -1.0, 1.0).astype(jnp.float32)
        block[...] = local[...]
        for t in range(tracers):
            m = recv[t] * sign
            for k in (0, 1):
                first = k * n_half + t * half_lev
                block[first : first + half_lev, :cols] += jnp.where(own == k, m[:half_lev], m[half_lev:])
        c, s = turned(dot3(block[...], fwd), turn, lon)
        keep[:, :half], keep[:, half:] = c[:n_half], s[:n_half]
        send[:, :half], send[:, half:] = c[n_half:], s[n_half:]
        at = KF % LANE
        spare = (cols + 2) // LANE * LANE
        lane = lax.broadcasted_iota(jnp.int32, (2 * n_half, LANE), 1)
        sums = pltpu.roll(local[:, spare : spare + LANE], (at - (cols + 2)) % LANE, 1)
        sums = jnp.where((lane >= at) & (lane < at + 3), sums, 0.0)
        keep[:, half - LANE : half] += sums[:n_half]
        send[:, half - LANE : half] += sums[n_half:]


def token_kernel(x, *rest):
    rest[-1][...] = x[:8, :LANE]


def sum_kernel(lat_count, mine, got, after, out):
    _, polar, _ = latitude_role(lat_count)

    @pl.when(polar)
    def _():
        out[...] = mine[...] + got[...]

    @pl.when(jnp.logical_not(polar))
    def _():
        out[:8] = got[:8]


def total_kernel(lat_count, mine, across, after, out):
    _, polar, _ = latitude_role(lat_count)

    @pl.when(polar)
    def _():
        out[...] = mine[...] + across[...]


def place(rows_ref, k, y, cols, half_lev):
    y = y.reshape(2, -1, half_lev, y.shape[-1])
    for h in (0, 1):
        rows_ref[k, :, h * half_lev : (h + 1) * half_lev, :] = y[h][..., :cols]


def pole_row(sums, t, half_lev, half, pole, lon, circle):
    p = sums[t * half_lev : (t + 1) * half_lev, half - LANE : half]
    at = KF % LANE
    c0, c1, s1 = p[:, at : at + 1], p[:, at + 1 : at + 2], p[:, at + 2 : at + 3]
    return (1.0 / circle) * c0 + (2.0 / circle) * (c1 * pole[lon, 1:2] + s1 * pole[lon, 2:3])


def cap_kernel(lat_count, circle, weights, mine, other, third, bwd, pole, out):
    _, tracers, levels, cols = out.shape
    half_lev = levels // 2
    n_half = tracers * half_lev
    half = bwd.shape[1] // 2
    _, polar, _ = latitude_role(lat_count)
    lon, own, _ = longitude_role()

    @pl.when(polar)
    def _():
        parts = (mine, own), (other, 1 - own)
        lev = pl.ds(pl.multiple_of(own * half_lev, half_lev), half_lev)
        for t in range(tracers):
            out[0, t, lev, :] = pole_row(third, t, half_lev, half, pole, lon, circle)[:, :cols]
        blocks = [
            weighted(source[slot * n_half : (slot + 1) * n_half], weights[slot]) for slot in range(2) for source, _ in parts
        ]
        blocks.append(weighted(third[...], weights[2]))
        y = dot3(jnp.concatenate(blocks), bwd)
        places = [(slot + 1, h) for slot in range(2) for _, h in parts] + [(3, own)]
        for k, (slot, h) in enumerate(places):
            lev = pl.ds(pl.multiple_of(h * half_lev, half_lev), half_lev)
            out[slot, :, lev, :] = y[k * n_half : (k + 1) * n_half, :cols].reshape(tracers, half_lev, cols)


def finish_kernel(
    lat_count, circle, weights, caps, base, recv_a, recv_b, from_core, from_x, third, bwd, pole, out, rows_ref, last_ref, pole_ref,
    sems,
):
    rows, tracers, levels, cols = base.shape
    half_lev = levels // 2
    south, polar, even = latitude_role(lat_count)
    lon, own, right_core = longitude_role()

    @pl.when(polar)
    def _():
        here, there = (pl.ds(pl.multiple_of(h * half_lev, half_lev), half_lev) for h in (own, 1 - own))
        top, row = jnp.where(south, rows - 1, 0), jnp.where(south, 0, rows - 1)
        moves = [(caps.at[near], out.at[jnp.where(south, rows - 1 - near, near)]) for near in range(1, rows - 1)]
        moves += [(caps.at[near, :, here, :], out.at[at, :, here, :]) for near, at in ((0, top), (rows - 1, row))]
        copies = []
        for k, (source, target) in enumerate(moves):
            copies.append(pltpu.make_async_copy(source, target, sems.at[k]))
            copies[-1].start()
        for t in range(tracers):
            pole_ref[t] = pole_row(third, t, half_lev, bwd.shape[1] // 2, pole, lon, circle)[:, :cols]
        copies.append(pltpu.make_async_copy(pole_ref, out.at[top, :, there, :], sems.at[rows + 1]))
        copies[-1].start()
        block = weighted(third[...], weights[2])
        middle = (cols // 2 + LANE - 1) // LANE * LANE
        for k, (first, end) in enumerate(((0, middle), (middle, cols))):
            y = dot3(block, bwd, first, middle)
            last_ref[:, :, first:end] = y[:, : end - first].reshape(tracers, half_lev, end - first)
            part = pl.ds(first, end - first)
            copies.append(
                pltpu.make_async_copy(
                    last_ref.at[:, :, part], out.at[row, :, there, part], sems.at[rows if k == 0 else rows + 2]
                )
            )
            copies[-1].start()
        for copy in copies:
            copy.wait()

    @pl.when(jnp.logical_not(polar))
    def _():
        row = lax.broadcasted_iota(jnp.int32, (8, LANE), 0)
        lane = lax.broadcasted_iota(jnp.int32, (8, LANE), 1)
        start = cols // LANE * LANE
        low = jnp.where((row == 1) & (lane == 0), 1.0, 0.0).astype(jnp.float32)
        high = jnp.where((row == 0) & (lane == cols - 1 - start), 1.0, 0.0).astype(jnp.float32)
        dims = (((0,), (0,)), ((), ()))
        exact = lax.Precision.HIGHEST
        count = rows * tracers * levels
        core_side, x_side = from_core[:8, :count], from_x[:8, :count]
        left = jnp.where(right_core, x_side, core_side)
        right = jnp.where(right_core, core_side, x_side)
        first = lax.dot_general(left, low, dims, precision=exact, preferred_element_type=jnp.float32)
        end = lax.dot_general(right, high, dims, precision=exact, preferred_element_type=jnp.float32)
        shape = (rows, tracers, levels, LANE)
        first, end = first.reshape(shape), end.reshape(shape)
        side_a = recv_a[...]
        side_b = recv_b[...]
        copies = []
        for r in range(rows):
            value = base[r]
            if r == rows - 1:
                value = value + jnp.where(even, side_a, side_b)
            if r == 0:
                value = value - jnp.where(even, side_b, side_a)
            rows_ref[r] = value
            rows_ref[r, :, :, :LANE] -= first[r]
            rows_ref[r, :, :, start:] += end[r][..., : cols - start]
            copies.append(pltpu.make_async_copy(rows_ref.at[r], out.at[r], sems.at[r]))
            copies[-1].start()
        for copy in copies:
            copy.wait()


def fast_body(adj, east, north, cutoff):
    lat_count, lon_count = lax.axis_size("lat"), lax.axis_size("lon")
    rows, tracers, levels, cols = adj.shape
    circle = cols * lon_count
    fwd, bwd, turn, pole = tables(cols, circle, lon_count)
    wide, width = fwd.shape[1:]
    last = lat_count - 1
    f32 = jnp.float32
    params = pltpu.CompilerParams(vmem_limit_bytes=40 << 20)
    dma = pltpu.SemaphoreType.DMA
    vmem = pl.BlockSpec(memory_space=VMEM)
    smem = pl.BlockSpec(memory_space=pltpu.SMEM)
    anywhere = pl.BlockSpec(memory_space=pl.ANY)
    far = pl.BlockSpec(memory_space=HBM)
    n_half = tracers * levels // 2
    pair, single = (2 * n_half, width), (n_half, width)
    half_row = (tracers, levels // 2, cols)

    def put(x, space):
        return pltpu.with_memory_space_constraint(x, space)

    def call(kernel, outs, *args, scratch=(), cost=LIGHT):
        return pl.pallas_call(
            functools.partial(kernel, lat_count),
            out_shape=[VMEM(s, f32) for s in outs],
            in_specs=[vmem] * len(args),
            out_specs=[vmem] * len(outs),
            scratch_shapes=[VMEM(s, f32) for s in scratch],
            compiler_params=params,
            cost_estimate=cost,
        )(*(put(x, VMEM) for x in args))

    lats, lons = range(lat_count), range(lon_count)

    def swap(x, pairs):
        return lax.ppermute(x, ("lat", "lon"), [(a * lon_count + i, b * lon_count + j) for a, i, b, j in pairs])

    by_core = [(a, i, a, i ^ 1) for a in lats for i in lons]
    by_x = [(a, i, a, i ^ 2) for a in lats for i in lons]
    by_lat = [(a, i, a ^ 1, i) for a in lats for i in lons]
    by_next = [(a, i, ((a + 1) ^ 1) - 1, i) for a in range(1, last) for i in lons]

    edge = pl.pallas_call(
        functools.partial(edge_kernel, lat_count),
        out_shape=VMEM(adj.shape[1:], f32),
        in_specs=[far] * 2,
        out_specs=vmem,
        scratch_shapes=[VMEM(adj.shape[1:], f32), VMEM(north.shape[1:], f32), dma((2,))],
        cost_estimate=HEAVY,
        compiler_params=params,
    )(put(adj, HBM), put(north, HBM))
    recv_a = swap(edge, by_lat)
    base, edge_b, keep, send = call(
        local_kernel,
        (adj.shape, adj.shape[1:], pair, pair),
        edge,
        adj,
        east,
        north,
        fwd,
        turn,
        scratch=((levels, wide), (rows - 2, 2, tracers, levels // 2, wide), (rows, tracers, levels, LANE)),
    )

    def token(*args):
        return pl.pallas_call(
            token_kernel,
            out_shape=VMEM((8, LANE), f32),
            in_specs=[vmem] * len(args),
            out_specs=vmem,
            compiler_params=params,
            cost_estimate=HEAVY,
        )(*(put(x, VMEM) for x in args))

    got = swap(send, by_core)
    weights, local = pl.pallas_call(
        functools.partial(side_kernel, lat_count, circle),
        out_shape=[VMEM((rows - 1, 2, width // 2), f32), VMEM((2 * n_half, wide), f32)],
        in_specs=[smem] + [vmem] * 6,
        out_specs=[vmem] * 2,
        scratch_shapes=[VMEM((4, tracers, levels, wide), f32)],
        compiler_params=params,
        cost_estimate=HEAVY,
    )(cutoff, *(put(x, VMEM) for x in (keep, adj, east, north, turn, pole)))
    (part,) = call(sum_kernel, (pair,), keep, got, weights)
    across = swap(part, by_x)
    recv_b = swap(edge_b, by_next)
    keep3, send3 = call(third_kernel, (single, single), local, recv_a, part, fwd, turn, scratch=((2 * n_half, wide),))
    got3 = swap(send3, by_core)
    (part3,) = call(sum_kernel, (single,), keep3, got3, send3)
    across3 = swap(part3, by_x)
    (mine,) = call(total_kernel, (pair,), part, across, part3)
    other = swap(mine, by_core)
    (mine3,) = call(total_kernel, (single,), part3, across3, token(part3, across, recv_b))
    other3 = swap(mine3, by_core)
    caps = pl.pallas_call(
        functools.partial(cap_kernel, lat_count, circle),
        out_shape=VMEM(adj.shape, f32),
        in_specs=[vmem] * 6,
        out_specs=vmem,
        compiler_params=params,
    )(*(put(x, VMEM) for x in (weights, mine, other, mine3, bwd, pole)))
    return pl.pallas_call(
        functools.partial(finish_kernel, lat_count, circle),
        out_shape=jax.ShapeDtypeStruct(adj.shape, f32),
        in_specs=[vmem] * 10,
        out_specs=anywhere,
        scratch_shapes=[VMEM(adj.shape, f32), VMEM(half_row, f32), VMEM(half_row, f32), dma((rows + 3,))],
        compiler_params=params,
    )(*(put(x, VMEM) for x in (weights, caps, base, recv_a, recv_b, got, across, other3, bwd, pole)))


full_precision = lax.Precision.HIGHEST


def extended(block, sides, width, periodic):
    for axis, dim in sides:
        count = lax.axis_size(axis)
        forward = [(i, i + 1) for i in range(count - 1)]
        if periodic:
            forward.append((count - 1, 0))
        backward = [(target, source) for source, target in forward]
        low = lax.ppermute(
            lax.slice_in_dim(block, block.shape[dim] - width, None, axis=dim), axis, forward
        )
        high = lax.ppermute(lax.slice_in_dim(block, 0, width, axis=dim), axis, backward)
        block = jnp.concatenate([low, block, high], axis=dim)
    return block


def from_partner(block, axis, stride):
    count = lax.axis_size(axis)
    route = []
    for low in range(count):
        high = low | 1 << stride
        if high != low and high < count:
            route += [(low, high), (high, low)]
    return lax.ppermute(block, axis, route)


def mode_table(columns, modes_kept, circle):
    wavenumber = jnp.arange(modes_kept, dtype=jnp.int32)
    product = columns[:, None] * wavenumber[None, :] % circle
    phases = product.astype(jnp.float32) * (2.0 * math.pi / circle)
    return jnp.concatenate([jnp.cos(phases), jnp.sin(phases)], axis=1)


def spectral_weights(latitude, cutoff, modes_kept, circle, total_lat):
    cap_lat = cutoff.shape[1]
    offsets = jnp.arange(cap_lat, dtype=jnp.int32)
    north_hit = latitude[..., None] == offsets
    south_hit = latitude[..., None] == total_lat - cap_lat + offsets
    chosen = jnp.sum(
        jnp.where(north_hit, cutoff[0], 0) + jnp.where(south_hit, cutoff[1], 0), axis=-1
    )
    wavenumber = jnp.arange(2 * modes_kept, dtype=jnp.int32) % modes_kept
    mode_weight = jnp.where(wavenumber == 0, 1.0, 2.0) / circle
    kept_mask = wavenumber <= chosen[..., None]
    return jnp.where(kept_mask, mode_weight, 0.0).astype(jnp.float32)


def general_body(adj_next, east_courant, north_courant, cutoff):
    lat_count = lax.axis_size("lat")
    lon_count = lax.axis_size("lon")
    lat_index = lax.axis_index("lat")
    lon_index = lax.axis_index("lon")
    lat_rows, tracers, levels, lon_cols = adj_next.shape
    circle = lon_cols * lon_count
    total_lat = lat_rows * lat_count
    modes_kept = KF
    cap_lat = cutoff.shape[1]
    zonal_flux = east_courant[:, None] * adj_next
    meridional = north_courant[:, None] * adj_next
    lon_padded = extended(zonal_flux, (("lon", 3),), 1, True)
    result = adj_next + lon_padded[..., 2:] - lon_padded[..., :-2]
    lat_padded = extended(meridional, (("lat", 0),), 1, False)
    result = result + lat_padded[2:] - lat_padded[:-2]
    edge_row = jnp.where(lat_index == 0, meridional[0], meridional[-1])
    pole_bit = lon_count.bit_length() - 2
    partner = from_partner(edge_row, "lon", pole_bit)
    north_sign = jnp.where(lat_index == 0, 1.0, 0.0).astype(jnp.float32)
    south_sign = jnp.where(lat_index == lat_count - 1, -1.0, 0.0).astype(jnp.float32)
    result = result.at[0].add(north_sign * partner)
    result = result.at[-1].add(south_sign * partner)
    latitude = lat_index * lat_rows + jnp.arange(lat_rows, dtype=jnp.int32)
    in_cap = (latitude < cap_lat) | (latitude >= total_lat - cap_lat)
    local_cols = lon_index * lon_cols + jnp.arange(lon_cols, dtype=jnp.int32)
    local_table = mode_table(local_cols, modes_kept, circle)
    weights = spectral_weights(latitude, cutoff, modes_kept, circle, total_lat)
    partial_sum = jnp.einsum(
        "acvn,nk->acvk",
        result,
        local_table,
        precision=full_precision,
        preferred_element_type=jnp.float32,
    )
    level_share = lax.psum_scatter(partial_sum, "lon", scatter_dimension=2, tiled=True)
    level_share = level_share * weights[:, None, None, :]
    totals = lax.all_gather(level_share, "lon", axis=2, tiled=True)
    rebuilt = jnp.einsum(
        "acvk,nk->acvn",
        totals,
        local_table,
        precision=full_precision,
        preferred_element_type=jnp.float32,
    )
    output = jnp.where(in_cap[:, None, None, None], rebuilt, result)
    return output


def body(adj, east, north, cutoff):
    lat_count, lon_count = lax.axis_size("lat"), lax.axis_size("lon")
    one_band = cutoff.shape[1] == adj.shape[0] == 4
    if one_band and lon_count == 4 and lat_count % 2 == 0 and lat_count >= 4 and adj.shape[2] % 16 == 0:
        return fast_body(adj, east, north, cutoff)
    return general_body(adj, east, north, cutoff)


def solution(mesh):
    return jax.shard_map(
        body,
        mesh=mesh,
        in_specs=(P("lat", None, None, "lon"), P("lat", None, "lon"), P("lat", None, "lon"), P()),
        out_specs=P("lat", None, None, "lon"),
        check_vma=False,
    )
```
